32 devices in a mesh: seq: 8 (over z, y), uly: 4 (over x, core).
Axes of the slice: x: 2, y: 2, z: 4, core: 2. Of those that a mesh axis runs over, the one named last changes fastest.
Arguments:
- queries: bfloat16 [4096, 5120], P(('seq', 'uly')), may hold values from -27 to 27
- keys: bfloat16 [4096, 5120], P(('seq', 'uly')), may hold values from -9 to 9
- values: bfloat16 [4096, 5120], P(('seq', 'uly')), may hold values from -6 to 6
- block_lists: int32 [32, 12], P('seq'), may hold values from 0 to 31, as said below
- block_counts: int32 [32], P('seq'), may hold values from 4 to 12
Outputs:
- attended: bfloat16 [4096, 5120], P(('seq', 'uly'))
The draws below stay inside these ranges and needn't reach their ends.
Inputs may be any that keep to these rules, and one draw needn't show every extreme that they name: `block_lists`: each row names 12 different blocks, its first entry being the query block itself; only the first block_counts entries of a row are used, the rest are block numbers too. Over the used entries of the 4 query blocks of one group (blocks g * 4 to (g + 1) * 4 - 1), at most 2 different blocks of any other group are named, and in every group exactly 2 of some other group.
All inputs are finite; a program needn't handle non-finite values.
Results may differ from the reference program's by a relative error of at most 0.003.
Values may be sent and summed in bfloat16 or wider, within the bound.
No kernel may reach another device: no remote copies, remote signals or barrier semaphores. Data moves between devices by JAX's collectives and lax.ppermute only.
A program may use at most 128 MiB of HBM per device.

```python
import jax
import jax.numpy as jnp
from jax import lax

NUM_HEADS = 40
HEAD_DIM = 128
BLOCK_LEN = 128
LIST_LEN = 12
PEER_SLOTS = 2
MODEL_WIDTH = 5120
TOKENS = 4096
GROUP_BLOCKS = 4
QBLOCKS = 32


def attention_inputs(key):
    base = jax.random.fold_in(key, 5)
    first, second = jax.random.split(base, 2)
    shape = (TOKENS, MODEL_WIDTH)
    query_part = jax.random.truncated_normal(first, -4.0, 4.0, shape) * 1.6
    key_part = jax.random.truncated_normal(second, -4.0, 4.0, shape) * 1.6
    return (query_part, key_part)


def draw_queries(key, part):
    return attention_inputs(key)[0].astype(jnp.bfloat16)


def draw_keys(key, part):
    return attention_inputs(key)[1].astype(jnp.bfloat16)


def mask_tables(key):
    base = jax.random.fold_in(key, 11)
    first, second, third, fourth = jax.random.split(base, 4)
    groups = QBLOCKS // GROUP_BLOCKS
    per_group = GROUP_BLOCKS
    order = jax.random.randint(first, (groups, groups, per_group), 0, 1 << 20) * per_group + jnp.arange(per_group, dtype=jnp.int32)
    picked = lax.top_k(order, PEER_SLOTS)[1].astype(jnp.int32)
    group_ids = jnp.arange(groups, dtype=jnp.int32)
    local_cands = group_ids[:, None] * per_group + jnp.arange(per_group, dtype=jnp.int32)[None, :]
    remote_cands = (group_ids[None, :, None] * per_group + picked).reshape(groups, groups * PEER_SLOTS)
    cands = jnp.concatenate([local_cands, remote_cands], axis=1)
    cand_width = per_group + groups * PEER_SLOTS
    block_ids = jnp.arange(QBLOCKS, dtype=jnp.int32)
    home_group = block_ids // per_group
    home_index = block_ids % per_group
    cand_index = jnp.arange(cand_width, dtype=jnp.int32)
    is_remote = cand_index[None, :] >= per_group
    cand_group = jnp.where(is_remote, (cand_index[None, :] - per_group) // PEER_SLOTS, home_group[:, None])
    score = jax.random.randint(second, (QBLOCKS, cand_width), 0, 1 << 20) * cand_width + cand_index[None, :]
    same_group = is_remote & (cand_group == home_group[:, None])
    own_block = (cand_index[None, :] == home_index[:, None]) & jnp.logical_not(is_remote)
    neighbour = (cand_index[None, :] == home_index[:, None] - 1) & (home_index[:, None] > 0) & jnp.logical_not(is_remote)
    next_group = is_remote & (cand_group == (home_group[:, None] + 1) % groups) & (home_index[:, None] == 0)
    score = score + jnp.where(own_block, 1 << 29, 0) + jnp.where(neighbour | next_group, 1 << 28, 0)
    score = jnp.where(same_group, cand_index[None, :] - cand_width, score)
    chosen = lax.top_k(score, LIST_LEN)[1].astype(jnp.int32)
    lists = jnp.take_along_axis(cands[home_group], chosen, axis=1).astype(jnp.int32)
    spread = jax.random.randint(third, (groups,), 6, LIST_LEN + 1)
    raw = jax.random.randint(fourth, (QBLOCKS,), 0, 1 << 20)
    counts = raw % (spread[home_group] - 3) + 4
    counts = jnp.where(block_ids == 0, LIST_LEN, jnp.where(block_ids == 1, 4, counts))
    return (lists, counts.astype(jnp.int32))


def draw_block_lists(key, part):
    return mask_tables(key)[0]


def draw_block_counts(key, part):
    return mask_tables(key)[1]


def shard_levels(rng, dims, cuts, low, largest):
    level = 1.0
    for dim, shards_of in cuts:
        steps = jax.random.uniform(jax.random.fold_in(jax.random.fold_in(rng, 6), dim), (shards_of,), jnp.float32, low / len(cuts), largest / len(cuts))
        level = level * jnp.repeat(jnp.exp(steps), dims[dim] // shards_of).reshape((-1,) + (1,) * (len(dims) - 1 - dim))
    return level


def noise(stream_key, dims, scale, limit, shards=(), held_as=jnp.bfloat16):
    values = scale * jax.random.normal(stream_key, dims, jnp.float32)
    if shards:
        values = values * shard_levels(stream_key, dims, shards, -0.22, 0.18)
    return jnp.clip(values, -limit, limit).astype(held_as)


def setup_inputs(seed: int = 0) -> dict:
    arg_keys = jax.random.split(jax.random.key(seed), 6)
    queries = draw_queries(jax.random.fold_in(arg_keys[5], 71), 0)
    keys = draw_keys(jax.random.fold_in(arg_keys[5], 71), 0)
    values = noise(arg_keys[2], (TOKENS, MODEL_WIDTH), 1.0, 6.0, ((0, 32),))
    block_lists = draw_block_lists(jax.random.fold_in(arg_keys[5], 71), 0)
    block_counts = draw_block_counts(jax.random.fold_in(arg_keys[5], 71), 0)
    return {"queries": queries, "keys": keys, "values": values, "block_lists": block_lists, "block_counts": block_counts}


def reference(queries, keys, values, block_lists, block_counts):
    token_count, feature_width = queries.shape
    query_blocks = queries.reshape(QBLOCKS, BLOCK_LEN, NUM_HEADS, HEAD_DIM)
    key_blocks = keys.reshape(QBLOCKS, BLOCK_LEN, NUM_HEADS, HEAD_DIM)
    value_blocks = values.reshape(QBLOCKS, BLOCK_LEN, NUM_HEADS, HEAD_DIM)
    score_scale = HEAD_DIM ** -0.5

    def attend(inputs):
        q_block, named_blocks, block_count = inputs
        key_part = jnp.take(key_blocks, named_blocks, axis=0).reshape(LIST_LEN * BLOCK_LEN, NUM_HEADS, HEAD_DIM)
        value_part = jnp.take(value_blocks, named_blocks, axis=0).reshape(LIST_LEN * BLOCK_LEN, NUM_HEADS, HEAD_DIM)
        scores = jnp.einsum("qhd,khd->hqk", q_block.astype(jnp.float32), key_part.astype(jnp.float32)) * score_scale
        live_keys = jnp.repeat(jnp.arange(LIST_LEN, dtype=jnp.int32) < block_count, BLOCK_LEN)
        scores = jnp.where(live_keys[None, None, :], scores, -jnp.inf)
        row_max = jnp.max(scores, axis=2, keepdims=True)
        weights = jnp.exp(scores - row_max)
        weight_sum = jnp.sum(weights, axis=2)
        rounded = lax.optimization_barrier(weights.astype(jnp.bfloat16)).astype(jnp.float32)
        blended = jnp.einsum("hqk,khd->qhd", rounded, value_part.astype(jnp.float32))
        result = blended / jnp.transpose(weight_sum)[:, :, None]
        return result.astype(jnp.bfloat16).reshape(BLOCK_LEN, NUM_HEADS * HEAD_DIM)

    attended = lax.map(attend, (query_blocks, block_lists, block_counts))
    return attended.reshape(token_count, feature_width)
```

```python
import functools
import math

import jax
import jax.numpy as jnp
from jax import lax
from jax.experimental import pallas as pl
from jax.experimental.pallas import tpu as pltpu
from jax.sharding import PartitionSpec as P

HEAD_DIM = 128
BLOCK_LEN = 128
LIST_LEN = 12
MIN_COUNT = 4
ROW = LIST_LEN + 1
VMEM_LIMIT = 56 * 1024 * 1024
CHUNK = 2
SCORE_FACTOR = HEAD_DIM**-0.5 * math.log2(math.e)
ANY = pl.BlockSpec(memory_space=pl.ANY)
SMEM = pl.BlockSpec(memory_space=pltpu.SMEM)
DEVICES = ("seq", "uly")


def swap(x, axis, bit):
    return lax.ppermute(x, axis, [(i, i ^ bit) for i in range(lax.axis_size(axis))])


def gather_all(x, axis):
    parts = {0: x}
    bit = lax.axis_size(axis) // 2
    while bit:
        parts.update({rel | bit: swap(part, axis, bit) for rel, part in list(parts.items())})
        bit //= 2
    return [parts[rel] for rel in range(lax.axis_size(axis))]


def gather_tables(block_lists, block_counts):
    table = jnp.concatenate([block_lists, block_counts[:, None]], axis=1).reshape(-1)
    bit = 1
    while bit < lax.axis_size("seq"):
        table = jnp.concatenate([table, swap(table, "seq", bit)])
        bit *= 2
    return table


def table_row(block, group_blocks):
    group = block // group_blocks
    return ((group ^ lax.axis_index("seq")) * group_blocks + block % group_blocks) * ROW


def pack_all_kernel(full, step, k_ref, v_ref, q_ref, out_ref):
    for d in range(step):
        for part, src in enumerate((k_ref, v_ref, q_ref)):
            for i in range(full):
                col = (d * full + i) * HEAD_DIM
                row = (part * full + i) * BLOCK_LEN
                out_ref[d, row : row + BLOCK_LEN] = src[:, col : col + HEAD_DIM]


def pack_all(queries, keys, values, full, devices):
    step = devices // 4
    block = pl.BlockSpec((BLOCK_LEN, step * full * HEAD_DIM), lambda j: (0, j))
    rows = 3 * full * BLOCK_LEN
    return pl.pallas_call(
        functools.partial(pack_all_kernel, full, step),
        grid=(devices // step,),
        out_shape=jax.ShapeDtypeStruct((devices, rows, HEAD_DIM), queries.dtype),
        in_specs=[block] * 3,
        out_specs=pl.BlockSpec((step, rows, HEAD_DIM), lambda j: (j, 0, 0)),
        cost_estimate=pl.CostEstimate(
            flops=0, transcendentals=0, bytes_accessed=devices * rows * HEAD_DIM * 4
        ),
        compiler_params=pltpu.CompilerParams(vmem_limit_bytes=VMEM_LIMIT),
        name="pack_all",
    )(keys, values, queries)


def pack_rest_kernel(head_axis, start, each, first, count, peers, k_ref, v_ref, q_ref, *refs):
    outs, bufs, sem = refs[:peers], refs[peers : peers + 3], refs[peers + 3]
    me = lax.axis_index(head_axis)
    width = peers * each * HEAD_DIM
    copies = [
        pltpu.make_async_copy(src.at[:, pl.ds(start * HEAD_DIM, width)], buf, sem)
        for src, buf in zip((k_ref, v_ref, q_ref), bufs)
    ]
    for copy in copies:
        copy.start()
    for copy in copies:
        copy.wait()
    for rel in range(peers):
        for part, buf in enumerate(bufs):
            for i in range(count):
                col = pl.multiple_of(((me ^ rel) * each + first + i) * HEAD_DIM, HEAD_DIM)
                row = (part * count + i) * BLOCK_LEN
                outs[rel][row : row + BLOCK_LEN] = buf[:, pl.ds(col, HEAD_DIM)]


def pack_rest(queries, keys, values, head_axis, start, each, first, count):
    peers = lax.axis_size(head_axis)
    rows = 3 * count * BLOCK_LEN
    return pl.pallas_call(
        functools.partial(pack_rest_kernel, head_axis, start, each, first, count, peers),
        out_shape=[jax.ShapeDtypeStruct((rows, HEAD_DIM), queries.dtype)] * peers,
        in_specs=[ANY] * 3,
        out_specs=[pl.BlockSpec(memory_space=pltpu.VMEM)] * peers,
        scratch_shapes=[pltpu.VMEM((BLOCK_LEN, peers * each * HEAD_DIM), queries.dtype)] * 3
        + [pltpu.SemaphoreType.DMA],
        cost_estimate=pl.CostEstimate(
            flops=0, transcendentals=0, bytes_accessed=peers * rows * HEAD_DIM * 4
        ),
        compiler_params=pltpu.CompilerParams(vmem_limit_bytes=VMEM_LIMIT),
        name="pack_rest",
    )(keys, values, queries)


def attend_block(q, pairs, used, write):
    def run(entries):
        keys, values = pairs(entries)
        over = jnp.where(used >= entries, 0.0, -jnp.inf).astype(jnp.float32)
        s = [
            lax.dot_general(q, k_e, (((1,), (1,)), ((), ())), preferred_element_type=jnp.float32)
            for k_e in keys
        ]
        s[-1] = s[-1] + over
        top = jnp.max(functools.reduce(jnp.maximum, s), axis=1, keepdims=True)
        w = [jnp.exp2((s_e - top) * SCORE_FACTOR) for s_e in s]
        total = jnp.sum(functools.reduce(jnp.add, w), axis=1, keepdims=True)
        blended = jnp.dot(
            jnp.concatenate([w_e.astype(jnp.bfloat16) for w_e in w], axis=1),
            jnp.concatenate(values, axis=0),
            preferred_element_type=jnp.float32,
        )
        write((blended * (1.0 / total)).astype(jnp.bfloat16))

    for entries in range(MIN_COUNT, LIST_LEN + 1, 2):
        pl.when((used == entries) | (used == entries - 1))(functools.partial(run, entries))


def attend_all_kernel(full, group_blocks, table, in_ref, out_ref, buf, o_buf, in_sem, out_sem):
    devices = in_ref.shape[0]
    copy = pltpu.make_async_copy(in_ref, buf, in_sem)
    copy.start()
    copy.wait()

    def step(block, carry):
        row = table_row(block, group_blocks)
        used = table[row + LIST_LEN]
        for i in range(full):
            own = pl.ds(i * BLOCK_LEN, BLOCK_LEN)

            def pairs(entries):
                named = [table[row + e] for e in range(entries)]
                keys = [buf[b, own] for b in named]
                return keys, [buf[b, pl.ds((full + i) * BLOCK_LEN, BLOCK_LEN)] for b in named]

            def write(result):
                o_buf[block, own] = result

            attend_block(buf[block, pl.ds((2 * full + i) * BLOCK_LEN, BLOCK_LEN)], pairs, used, write)
        pltpu.make_async_copy(o_buf.at[block], out_ref.at[block], out_sem).start()
        return carry

    lax.fori_loop(0, devices, step, 0)
    pltpu.make_async_copy(o_buf, out_ref, out_sem).wait()


def attend_cost(blocks, heads, in_bytes):
    pairs = blocks * heads * LIST_LEN
    return pl.CostEstimate(
        flops=pairs * 4 * BLOCK_LEN * BLOCK_LEN * HEAD_DIM,
        transcendentals=pairs * BLOCK_LEN * BLOCK_LEN,
        bytes_accessed=in_bytes,
    )


def attend_all(table, arrived, full, group_blocks):
    devices = arrived.shape[0]
    shape = (devices, full * BLOCK_LEN, HEAD_DIM)
    return pl.pallas_call(
        functools.partial(attend_all_kernel, full, group_blocks),
        out_shape=jax.ShapeDtypeStruct(shape, jnp.bfloat16),
        in_specs=[SMEM, ANY],
        out_specs=ANY,
        scratch_shapes=[
            pltpu.VMEM(arrived.shape, jnp.bfloat16),
            pltpu.VMEM(shape, jnp.bfloat16),
            pltpu.SemaphoreType.DMA,
            pltpu.SemaphoreType.DMA,
        ],
        compiler_params=pltpu.CompilerParams(vmem_limit_bytes=VMEM_LIMIT),
        cost_estimate=attend_cost(devices, full, arrived.size * 2),
        name="attend_all",
    )(table, arrived)


def attend_rest_kernel(head_axis, gather_axis, count, peers, others, group_blocks, table, *refs):
    pieces, refs = refs[:peers], refs[peers:]
    gathered, refs = refs[:others], refs[others:]
    outs, refs = refs[:peers], refs[peers:]
    q_buf, kv_buf, o_buf, in_sem, out_sem = refs
    part_rows = count * BLOCK_LEN
    copies = [
        pltpu.make_async_copy(pieces[r].at[pl.ds(2 * part_rows, part_rows)], q_buf.at[r], in_sem)
        for r in range(peers)
    ]
    copies += [
        pltpu.make_async_copy(gathered[g], kv_buf.at[pl.ds(g * peers, peers)], in_sem)
        for g in range(others)
    ]
    for copy in copies:
        copy.start()
    for copy in copies:
        copy.wait()
    my_head, my_gather = lax.axis_index(head_axis), lax.axis_index(gather_axis)
    inner = lax.axis_size("uly")
    outer_heads = head_axis == "seq"

    def place(block):
        outer, low = block // inner, block % inner
        h, g = (outer, low) if outer_heads else (low, outer)
        return (g ^ my_gather) * peers + (h ^ my_head)

    def step(r, carry):
        h = my_head ^ r
        block = h * inner + my_gather if outer_heads else my_gather * inner + h
        row = table_row(block, group_blocks)
        used = table[row + LIST_LEN]
        for i in range(count):
            own = pl.ds(i * BLOCK_LEN, BLOCK_LEN)

            def pairs(entries):
                slots = [place(table[row + e]) for e in range(entries)]
                keys = [kv_buf[slot, own] for slot in slots]
                return keys, [kv_buf[slot, pl.ds((count + i) * BLOCK_LEN, BLOCK_LEN)] for slot in slots]

            def write(result):
                o_buf[r, own] = result

            attend_block(q_buf[r, own], pairs, used, write)
        return carry

    lax.fori_loop(0, peers, step, 0)
    copies = [pltpu.make_async_copy(o_buf.at[r], outs[r], out_sem) for r in range(peers)]
    for copy in copies:
        copy.start()
    for copy in copies:
        copy.wait()


def attend_rest(table, pieces, gathered, head_axis, gather_axis, count, group_blocks):
    peers, others = len(pieces), len(gathered)
    part_rows = count * BLOCK_LEN
    return pl.pallas_call(
        functools.partial(
            attend_rest_kernel, head_axis, gather_axis, count, peers, others, group_blocks
        ),
        out_shape=[jax.ShapeDtypeStruct((part_rows, HEAD_DIM), jnp.bfloat16)] * peers,
        in_specs=[SMEM] + [ANY] * (peers + others),
        out_specs=[ANY] * peers,
        scratch_shapes=[
            pltpu.VMEM((peers, part_rows, HEAD_DIM), jnp.bfloat16),
            pltpu.VMEM((others * peers, 2 * part_rows, HEAD_DIM), jnp.bfloat16),
            pltpu.VMEM((peers, part_rows, HEAD_DIM), jnp.bfloat16),
            pltpu.SemaphoreType.DMA,
            pltpu.SemaphoreType.DMA,
        ],
        compiler_params=pltpu.CompilerParams(vmem_limit_bytes=VMEM_LIMIT),
        cost_estimate=attend_cost(peers, count, peers * (others + 1) * 2 * part_rows * HEAD_DIM * 2),
        name="attend_rest",
    )(table, *pieces, *gathered)


def unpack_kernel(head_axis, start, each, full, chunks, peers, devices, *refs):
    has_main = 1 if full else 0
    n = has_main + len(chunks) * peers
    parts, out_ref, buf, in_sem, out_sem = refs[:n], refs[n], refs[n + 1], refs[n + 2], refs[n + 3]
    me = lax.axis_index(head_axis)
    copies = []
    for d in range(devices * has_main):
        for i in range(full):
            copies.append(
                pltpu.make_async_copy(
                    parts[0].at[d, pl.ds(i * BLOCK_LEN, BLOCK_LEN)],
                    buf.at[:, pl.ds((d * full + i) * HEAD_DIM, HEAD_DIM)],
                    in_sem,
                )
            )
    for j, (first, count) in enumerate(chunks):
        for rel in range(peers):
            for i in range(count):
                col = pl.multiple_of((start + (me ^ rel) * each + first + i) * HEAD_DIM, HEAD_DIM)
                copies.append(
                    pltpu.make_async_copy(
                        parts[has_main + j * peers + rel].at[pl.ds(i * BLOCK_LEN, BLOCK_LEN)],
                        buf.at[:, pl.ds(col, HEAD_DIM)],
                        in_sem,
                    )
                )
    for copy in copies:
        copy.start()
    for copy in copies:
        copy.wait()
    copy = pltpu.make_async_copy(buf, out_ref, out_sem)
    copy.start()
    copy.wait()


def unpack(parts, head_axis, start, each, full, chunks, devices, width):
    peers = lax.axis_size(head_axis)
    return pl.pallas_call(
        functools.partial(unpack_kernel, head_axis, start, each, full, chunks, peers, devices),
        out_shape=jax.ShapeDtypeStruct((BLOCK_LEN, width), jnp.bfloat16),
        in_specs=[ANY] * len(parts),
        out_specs=ANY,
        scratch_shapes=[
            pltpu.VMEM((BLOCK_LEN, width), jnp.bfloat16),
            pltpu.SemaphoreType.DMA,
            pltpu.SemaphoreType.DMA,
        ],
        cost_estimate=pl.CostEstimate(
            flops=0, transcendentals=0, bytes_accessed=2 * BLOCK_LEN * width * 2
        ),
        compiler_params=pltpu.CompilerParams(vmem_limit_bytes=VMEM_LIMIT),
        name="unpack",
    )(*parts)


def body(queries, keys, values, block_lists, block_counts):
    width = queries.shape[1]
    heads = width // HEAD_DIM
    devices = lax.axis_size(DEVICES)
    group_blocks = block_lists.shape[0]
    assert queries.shape[0] == BLOCK_LEN
    full = heads // devices
    start = full * devices
    head_axis, gather_axis = "seq", "uly"
    if (heads - start) % lax.axis_size(head_axis):
        head_axis, gather_axis = gather_axis, head_axis
    peers = lax.axis_size(head_axis)
    each = (heads - start) // peers
    chunks = tuple((first, min(CHUNK, each - first)) for first in range(0, each, CHUNK))
    half = peers // 2
    order = [rel for pair in zip(range(half, peers), range(half)) for rel in pair if rel]

    def exchange(parts):
        moved = {rel: swap(parts[rel], head_axis, rel) for rel in order}
        return [parts[0]] + [moved[rel] for rel in range(1, peers)]

    results = []
    if full:
        sent = pack_all(queries, keys, values, full, devices)
        arrived = lax.all_to_all(sent, DEVICES, split_axis=0, concat_axis=0, tiled=True)
    table = gather_tables(block_lists, block_counts)
    inputs = []
    for first, count in chunks:
        inputs.append(exchange(pack_rest(queries, keys, values, head_axis, start, each, first, count)))
    if full:
        blended = attend_all(table, arrived, full, group_blocks)
        results.append(lax.all_to_all(blended, DEVICES, split_axis=0, concat_axis=0, tiled=True))
    for (first, count), pieces in zip(chunks, inputs):
        kv = jnp.stack([piece[: 2 * count * BLOCK_LEN] for piece in pieces])
        gathered = gather_all(kv, gather_axis)
        outs = attend_rest(table, pieces, gathered, head_axis, gather_axis, count, group_blocks)
        results.extend(exchange(outs))
    return unpack(results, head_axis, start, each, full, chunks, devices, width)


def solution(mesh):
    rows = P(DEVICES, None)
    placed = (rows, rows, rows, P("seq", None), P("seq"))
    return jax.shard_map(body, mesh=mesh, in_specs=placed, out_specs=rows, check_vma=False)
```

```python
import functools
import math

import jax
import jax.numpy as jnp
from jax import lax
from jax.experimental import pallas as pl
from jax.experimental.pallas import tpu as pltpu
from jax.sharding import PartitionSpec as P

HEAD_DIM = 128
BLOCK_LEN = 128
LIST_LEN = 12
MIN_COUNT = 4
ROW = LIST_LEN + 1
MIB = 1024 * 1024
CHUNK = 2
TOGETHER = 4
TABLE_ROWS = 16
IN_FLIGHT = 5
TIED = 7
SCORE_FACTOR = HEAD_DIM**-0.5 * math.log2(math.e)
ANY = pl.BlockSpec(memory_space=pl.ANY)
SMEM = pl.BlockSpec(memory_space=pltpu.SMEM)
DEVICES = ("seq", "uly")


def swap(x, axis, bit):
    return lax.ppermute(x, axis, [(i, i ^ bit) for i in range(lax.axis_size(axis))])


def gather_all(x, axis):
    parts = {0: x}
    bit = lax.axis_size(axis) // 2
    while bit:
        parts.update({rel | bit: swap(part, axis, bit) for rel, part in list(parts.items())})
        bit //= 2
    return [parts[rel] for rel in range(lax.axis_size(axis))]


def row_of(block, head_axis, gather_axis):
    inner = lax.axis_size("uly")
    outer, low = block // inner, block % inner
    head, other = (outer, low) if head_axis == "seq" else (low, outer)
    return (other ^ lax.axis_index(gather_axis)) * lax.axis_size(head_axis) + (
        head ^ lax.axis_index(head_axis)
    )


def pack_all_kernel(full, step, k_ref, v_ref, q_ref, out_ref):
    for d in range(step):
        for part, src in enumerate((k_ref, v_ref, q_ref)):
            for i in range(full):
                col = (d * full + i) * HEAD_DIM
                row = (part * full + i) * BLOCK_LEN
                out_ref[d, row : row + BLOCK_LEN] = src[:, col : col + HEAD_DIM]


def pack_all(queries, keys, values, full, devices):
    step = devices // 4
    block = pl.BlockSpec((BLOCK_LEN, step * full * HEAD_DIM), lambda j: (0, j))
    rows = 3 * full * BLOCK_LEN
    return pl.pallas_call(
        functools.partial(pack_all_kernel, full, step),
        grid=(devices // step,),
        out_shape=jax.ShapeDtypeStruct((devices, rows, HEAD_DIM), queries.dtype),
        in_specs=[block] * 3,
        out_specs=pl.BlockSpec((step, rows, HEAD_DIM), lambda j: (j, 0, 0)),
        cost_estimate=pl.CostEstimate(
            flops=0, transcendentals=0, bytes_accessed=devices * rows * HEAD_DIM * 4
        ),
        compiler_params=pltpu.CompilerParams(vmem_limit_bytes=56 * MIB),
        name="pack_all",
    )(keys, values, queries)


def pack_rest_kernel(head_axis, start, each, first, count, peers, lists, counts, k_ref, v_ref, q_ref, *refs):
    outs, bufs, sem = refs[:peers], refs[peers : peers + 3], refs[peers + 3]
    me, mine = lax.axis_index(head_axis), lax.axis_index("uly")
    width = peers * each * HEAD_DIM
    copies = [
        pltpu.make_async_copy(src.at[:, pl.ds(start * HEAD_DIM, width)], buf, sem)
        for src, buf in zip((k_ref, v_ref, q_ref), bufs)
    ]
    for copy in copies:
        copy.start()
    lane = lax.broadcasted_iota(jnp.int32, (TABLE_ROWS, HEAD_DIM), 1)
    table = jnp.where(lane == LIST_LEN, counts[mine], 0)
    for e in range(LIST_LEN):
        table = jnp.where(lane == e, lists[mine, e], table)
    table = table.astype(jnp.float32).astype(jnp.bfloat16)
    for copy in copies:
        copy.wait()
    for rel in range(peers):
        for part, buf in enumerate(bufs):
            for i in range(count):
                col = pl.multiple_of(((me ^ rel) * each + first + i) * HEAD_DIM, HEAD_DIM)
                row = (part * count + i) * BLOCK_LEN + (part == 2) * TABLE_ROWS
                outs[rel][row : row + BLOCK_LEN] = buf[:, pl.ds(col, HEAD_DIM)]
        row = 2 * count * BLOCK_LEN
        outs[rel][row : row + TABLE_ROWS] = table


def pack_rest(queries, keys, values, lists, counts, head_axis, start, each, first, count):
    peers = lax.axis_size(head_axis)
    rows = 3 * count * BLOCK_LEN + TABLE_ROWS
    return pl.pallas_call(
        functools.partial(pack_rest_kernel, head_axis, start, each, first, count, peers),
        out_shape=[jax.ShapeDtypeStruct((rows, HEAD_DIM), queries.dtype)] * peers,
        in_specs=[SMEM] * 2 + [ANY] * 3,
        out_specs=[pl.BlockSpec(memory_space=pltpu.VMEM)] * peers,
        scratch_shapes=[pltpu.VMEM((BLOCK_LEN, peers * each * HEAD_DIM), queries.dtype)] * 3
        + [pltpu.SemaphoreType.DMA],
        cost_estimate=pl.CostEstimate(
            flops=0, transcendentals=0, bytes_accessed=peers * rows * HEAD_DIM * 4
        ),
        compiler_params=pltpu.CompilerParams(vmem_limit_bytes=56 * MIB),
        name="pack_rest",
    )(lists, counts, keys, values, queries)


def attend_blocks(queries, useds, pairs, write):
    most = functools.reduce(jnp.maximum, useds)

    def run(entries):
        scores, values = [], []
        for t, q in enumerate(queries):
            k, v = pairs(t, entries)
            s = []
            for e in range(0, entries, 2):
                both = lax.dot_general(
                    q,
                    jnp.concatenate(k[e : e + 2], axis=0),
                    (((1,), (1,)), ((), ())),
                    preferred_element_type=jnp.float32,
                )
                s += [both[:, :BLOCK_LEN], both[:, BLOCK_LEN:]]
            for e in range(MIN_COUNT, entries):
                s[e] = s[e] + jnp.where(useds[t] > e, 0.0, -jnp.inf).astype(jnp.float32)
            scores.append(s)
            values.append(v)
        for t, (s, v) in enumerate(zip(scores, values)):
            top = jnp.max(functools.reduce(jnp.maximum, s), axis=1, keepdims=True)
            w = [jnp.exp2((s_e - top) * SCORE_FACTOR) for s_e in s]
            total = jnp.sum(functools.reduce(jnp.add, w), axis=1, keepdims=True)
            blended = jnp.dot(
                jnp.concatenate([w_e.astype(jnp.bfloat16) for w_e in w], axis=1),
                jnp.concatenate(v, axis=0),
                preferred_element_type=jnp.float32,
            )
            write(t, (blended * (1.0 / total)).astype(jnp.bfloat16))

    for entries in range(MIN_COUNT, LIST_LEN + 1, 2):
        pl.when((most == entries) | (most == entries - 1))(functools.partial(run, entries))


def attend_all_kernel(full, place, table, in_ref, out_ref, buf, o_buf, in_sem, out_sem):
    devices = in_ref.shape[0]
    copy = pltpu.make_async_copy(in_ref, buf, in_sem)
    copy.start()
    copy.wait()

    def step(j, carry):
        blocks = [j * TOGETHER + t for t in range(TOGETHER)]
        rows = [place(block) * ROW for block in blocks]
        useds = [table[row + LIST_LEN] for row in rows]
        for i in range(full):
            own = pl.ds(i * BLOCK_LEN, BLOCK_LEN)

            def pairs(t, entries):
                named = [table[rows[t] + e] for e in range(entries)]
                keys = [buf[b, own] for b in named]
                return keys, [buf[b, pl.ds((full + i) * BLOCK_LEN, BLOCK_LEN)] for b in named]

            def write(t, result):
                o_buf[blocks[t], own] = result

            queries = [buf[b, pl.ds((2 * full + i) * BLOCK_LEN, BLOCK_LEN)] for b in blocks]
            attend_blocks(queries, useds, pairs, write)
        done = pl.ds(j * TOGETHER, TOGETHER)
        pltpu.make_async_copy(o_buf.at[done], out_ref.at[done], out_sem).start()
        return carry

    lax.fori_loop(0, devices // TOGETHER, step, 0)
    pltpu.make_async_copy(o_buf, out_ref, out_sem).wait()


def attend_cost(blocks, heads, in_bytes):
    pairs = blocks * heads * LIST_LEN
    return pl.CostEstimate(
        flops=pairs * 4 * BLOCK_LEN * BLOCK_LEN * HEAD_DIM,
        transcendentals=pairs * BLOCK_LEN * BLOCK_LEN,
        bytes_accessed=in_bytes,
    )


def attend_all(table, arrived, full, place):
    devices = arrived.shape[0]
    shape = (devices, full * BLOCK_LEN, HEAD_DIM)
    return pl.pallas_call(
        functools.partial(attend_all_kernel, full, place),
        out_shape=jax.ShapeDtypeStruct(shape, jnp.bfloat16),
        in_specs=[SMEM, ANY],
        out_specs=ANY,
        scratch_shapes=[
            pltpu.VMEM(arrived.shape, jnp.bfloat16),
            pltpu.VMEM(shape, jnp.bfloat16),
            pltpu.SemaphoreType.DMA,
            pltpu.SemaphoreType.DMA,
        ],
        compiler_params=pltpu.CompilerParams(vmem_limit_bytes=16 * MIB),
        cost_estimate=attend_cost(devices, full, arrived.size * 2),
        name="attend_all",
    )(table, arrived)


def stack_kernel(peers, rows, *refs):
    pieces, out_ref, sem = refs[:peers], refs[peers], refs[peers + 1]
    copies = [
        pltpu.make_async_copy(piece.at[pl.ds(0, rows)], out_ref.at[rel], sem)
        for rel, piece in enumerate(pieces)
    ]
    for copy in copies:
        copy.start()
    for copy in copies:
        copy.wait()


def stack(pieces, rows):
    shape = (len(pieces), rows, HEAD_DIM)
    return pl.pallas_call(
        functools.partial(stack_kernel, len(pieces), rows),
        out_shape=jax.ShapeDtypeStruct(shape, jnp.bfloat16),
        in_specs=[ANY] * len(pieces),
        out_specs=pl.BlockSpec(memory_space=pltpu.VMEM),
        scratch_shapes=[pltpu.SemaphoreType.DMA],
        cost_estimate=pl.CostEstimate(flops=0, transcendentals=0, bytes_accessed=4 * math.prod(shape)),
        compiler_params=pltpu.CompilerParams(vmem_limit_bytes=12 * MIB),
        name="stack",
    )(*pieces)


def attend_rest_kernel(head_axis, gather_axis, count, peers, others, place, table, *refs):
    pieces, refs = refs[:peers], refs[peers:]
    gathered, refs = refs[:others], refs[others:]
    outs, refs = refs[:peers], refs[peers:]
    q_buf, kv_buf, o_buf, in_sem, out_sem = refs
    part_rows = count * BLOCK_LEN
    copies = [
        pltpu.make_async_copy(piece.at[pl.ds(2 * part_rows + TABLE_ROWS, part_rows)], q_buf.at[rel], in_sem)
        for rel, piece in enumerate(pieces)
    ]
    copies += [
        pltpu.make_async_copy(part.at[:, pl.ds(0, 2 * part_rows)], kv_buf.at[pl.ds(g * peers, peers)], in_sem)
        for g, part in enumerate(gathered)
    ]
    for copy in copies:
        copy.start()
    for copy in copies:
        copy.wait()
    my_head, my_gather = lax.axis_index(head_axis), lax.axis_index(gather_axis)
    inner = lax.axis_size("uly")

    def step(j, carry):
        mine = [j * TOGETHER + t for t in range(TOGETHER)]
        heads = [my_head ^ rel for rel in mine]
        blocks = [h * inner + my_gather if head_axis == "seq" else my_gather * inner + h for h in heads]
        rows = [place(block) * ROW for block in blocks]
        useds = [table[row + LIST_LEN] for row in rows]
        for i in range(count):
            own = pl.ds(i * BLOCK_LEN, BLOCK_LEN)

            def pairs(t, entries):
                slots = [place(table[rows[t] + e]) for e in range(entries)]
                keys = [kv_buf[slot, own] for slot in slots]
                return keys, [kv_buf[slot, pl.ds((count + i) * BLOCK_LEN, BLOCK_LEN)] for slot in slots]

            def write(t, result):
                o_buf[mine[t], own] = result

            attend_blocks([q_buf[r, own] for r in mine], useds, pairs, write)
        return carry

    lax.fori_loop(0, peers // TOGETHER, step, 0)
    copies = [
        pltpu.make_async_copy(o_buf.at[rel], outs[rel], out_sem) for rel in range(peers)
    ]
    for copy in copies:
        copy.start()
    for copy in copies:
        copy.wait()


def attend_rest(table, pieces, gathered, head_axis, gather_axis, count, place):
    peers, others = lax.axis_size(head_axis), lax.axis_size(gather_axis)
    part_rows = count * BLOCK_LEN
    kv_shape = (others * peers, 2 * part_rows, HEAD_DIM)
    return pl.pallas_call(
        functools.partial(attend_rest_kernel, head_axis, gather_axis, count, peers, others, place),
        out_shape=[jax.ShapeDtypeStruct((part_rows, HEAD_DIM), jnp.bfloat16)] * peers,
        in_specs=[SMEM] + [ANY] * (peers + others),
        out_specs=[ANY] * peers,
        scratch_shapes=[
            pltpu.VMEM((peers, part_rows, HEAD_DIM), jnp.bfloat16),
            pltpu.VMEM(kv_shape, jnp.bfloat16),
            pltpu.VMEM((peers, part_rows, HEAD_DIM), jnp.bfloat16),
            pltpu.SemaphoreType.DMA,
            pltpu.SemaphoreType.DMA,
        ],
        compiler_params=pltpu.CompilerParams(vmem_limit_bytes=2 * math.prod(kv_shape) + 12 * MIB),
        cost_estimate=attend_cost(peers, count, 2 * math.prod(kv_shape)),
        name="attend_rest",
    )(table, *pieces, *gathered)


def unpack_kernel(head_axis, start, each, full, chunks, peers, devices, *refs):
    has_main = 1 if full else 0
    n = has_main + len(chunks) * peers
    parts, out_ref, buf, in_sem, out_sem = refs[:n], refs[n], refs[n + 1], refs[n + 2], refs[n + 3]
    me = lax.axis_index(head_axis)
    copies = []
    for d in range(devices * has_main):
        for i in range(full):
            copies.append(
                pltpu.make_async_copy(
                    parts[0].at[d, pl.ds(i * BLOCK_LEN, BLOCK_LEN)],
                    buf.at[:, pl.ds((d * full + i) * HEAD_DIM, HEAD_DIM)],
                    in_sem,
                )
            )
    for j, (first, count) in enumerate(chunks):
        for rel in range(peers):
            for i in range(count):
                col = pl.multiple_of((start + (me ^ rel) * each + first + i) * HEAD_DIM, HEAD_DIM)
                copies.append(
                    pltpu.make_async_copy(
                        parts[has_main + j * peers + rel].at[pl.ds(i * BLOCK_LEN, BLOCK_LEN)],
                        buf.at[:, pl.ds(col, HEAD_DIM)],
                        in_sem,
                    )
                )
    for copy in copies:
        copy.start()
    for copy in copies:
        copy.wait()
    copy = pltpu.make_async_copy(buf, out_ref, out_sem)
    copy.start()
    copy.wait()


def unpack(parts, head_axis, start, each, full, chunks, devices, width):
    peers = lax.axis_size(head_axis)
    return pl.pallas_call(
        functools.partial(unpack_kernel, head_axis, start, each, full, chunks, peers, devices),
        out_shape=jax.ShapeDtypeStruct((BLOCK_LEN, width), jnp.bfloat16),
        in_specs=[ANY] * len(parts),
        out_specs=ANY,
        scratch_shapes=[
            pltpu.VMEM((BLOCK_LEN, width), jnp.bfloat16),
            pltpu.SemaphoreType.DMA,
            pltpu.SemaphoreType.DMA,
        ],
        cost_estimate=pl.CostEstimate(
            flops=0, transcendentals=0, bytes_accessed=2 * BLOCK_LEN * width * 2
        ),
        compiler_params=pltpu.CompilerParams(vmem_limit_bytes=8 * MIB),
        name="unpack",
    )(*parts)


def body(queries, keys, values, block_lists, block_counts):
    width = queries.shape[1]
    heads = width // HEAD_DIM
    devices = lax.axis_size(DEVICES)
    assert queries.shape[0] == BLOCK_LEN
    full = heads // devices
    start = full * devices
    head_axis, gather_axis = "seq", "uly"
    if (heads - start) % lax.axis_size(head_axis):
        head_axis, gather_axis = gather_axis, head_axis
    peers = lax.axis_size(head_axis)
    each = (heads - start) // peers
    chunks = tuple((first, min(CHUNK, each - first)) for first in range(0, each, CHUNK))
    half = peers // 2
    order = [rel for pair in zip(range(half, peers), [1, *range(2, half), 0]) for rel in pair if rel]
    place = functools.partial(row_of, head_axis=head_axis, gather_axis=gather_axis)
    assert devices <= 256

    arrivals, tied = [], []
    for first, count in chunks:
        sends = pack_rest(
            queries, keys, values, block_lists, block_counts, head_axis, start, each, first, count
        )
        queries, keys, values, sends = lax.optimization_barrier((queries, keys, values, sends))
        moved = {rel: swap(sends[rel], head_axis, rel) for rel in order}
        tied.extend(moved[rel] for rel in order[:TIED])
        arrivals.append([sends[0]] + [moved[rel] for rel in range(1, peers)])
    if full:
        sent = pack_all(queries, keys, values, full, devices)
        sent, _ = lax.optimization_barrier((sent, tied))
        arrived = lax.all_to_all(sent, DEVICES, split_axis=0, concat_axis=0, tiled=True)
    outputs, table = [], None
    for (first, count), pieces in zip(chunks, arrivals):
        kv_rows = 2 * count * BLOCK_LEN
        gathered = gather_all(stack(pieces, kv_rows + TABLE_ROWS), gather_axis)
        if table is None:
            table = jnp.concatenate([part[:, kv_rows, :ROW] for part in gathered])
            table = table.astype(jnp.int32).reshape(-1)
        outputs.append(attend_rest(table, pieces, gathered, head_axis, gather_axis, count, place))
    results, backs = [], []
    if full:
        arrived, _ = lax.optimization_barrier((arrived, outputs))
        blended = attend_all(table, arrived, full, place)
    for outs in outputs:
        late = list(range(half, peers)) + list(range(half - 1, 0, -1))
        moved = {rel: swap(outs[rel], head_axis, rel) for rel in late}
        if full:
            early = late[:IN_FLIGHT]
            blended, kept = lax.optimization_barrier((blended, [moved[rel] for rel in early]))
            moved.update(zip(early, kept))
        backs.extend([outs[0]] + [moved[rel] for rel in range(1, peers)])
    if full:
        results.append(lax.all_to_all(blended, DEVICES, split_axis=0, concat_axis=0, tiled=True))
    results.extend(backs)
    return unpack(results, head_axis, start, each, full, chunks, devices, width)


def solution(mesh):
    rows = P(DEVICES, None)
    placed = (rows, rows, rows, P("seq", None), P("seq"))
    return jax.shard_map(body, mesh=mesh, in_specs=placed, out_specs=rows, check_vma=False)
```

```python
import functools
import math

import jax
import jax.numpy as jnp
from jax import lax
from jax.experimental import pallas as pl
from jax.experimental.pallas import tpu as pltpu
from jax.sharding import PartitionSpec as P

HEAD_DIM = 128
BLOCK_LEN = 128
LIST_LEN = 12
MIN_COUNT = 4
ROW = LIST_LEN + 1
MIB = 1024 * 1024
CHUNK = 2
TOGETHER = 4
TABLE_ROWS = 16
IN_FLIGHT = 5
TIED = 7
SCORE_FACTOR = HEAD_DIM**-0.5 * math.log2(math.e)
ANY = pl.BlockSpec(memory_space=pl.ANY)
SMEM = pl.BlockSpec(memory_space=pltpu.SMEM)
HBM = pl.BlockSpec(memory_space=pltpu.HBM)
DEVICES = ("seq", "uly")


def swap(x, axis, bit):
    return lax.ppermute(x, axis, [(i, i ^ bit) for i in range(lax.axis_size(axis))])


def gather_all(x, axis):
    parts = {0: x}
    bit = lax.axis_size(axis) // 2
    while bit:
        parts.update({rel | bit: swap(part, axis, bit) for rel, part in list(parts.items())})
        bit //= 2
    return [parts[rel] for rel in range(lax.axis_size(axis))]


def row_of(block, head_axis, gather_axis):
    inner = lax.axis_size("uly")
    outer, low = block // inner, block % inner
    head, other = (outer, low) if head_axis == "seq" else (low, outer)
    return (other ^ lax.axis_index(gather_axis)) * lax.axis_size(head_axis) + (
        head ^ lax.axis_index(head_axis)
    )


def pack_all_kernel(full, step, k_ref, v_ref, q_ref, out_ref):
    for d in range(step):
        for part, src in enumerate((k_ref, v_ref, q_ref)):
            for i in range(full):
                col = (d * full + i) * HEAD_DIM
                row = (part * full + i) * BLOCK_LEN
                out_ref[d, row : row + BLOCK_LEN] = src[:, col : col + HEAD_DIM]


def pack_all(queries, keys, values, full, devices):
    step = devices // 4
    block = pl.BlockSpec((BLOCK_LEN, step * full * HEAD_DIM), lambda j: (0, j))
    rows = 3 * full * BLOCK_LEN
    return pl.pallas_call(
        functools.partial(pack_all_kernel, full, step),
        grid=(devices // step,),
        out_shape=jax.ShapeDtypeStruct((devices, rows, HEAD_DIM), queries.dtype),
        in_specs=[block] * 3,
        out_specs=pl.BlockSpec((step, rows, HEAD_DIM), lambda j: (j, 0, 0)),
        cost_estimate=pl.CostEstimate(
            flops=0, transcendentals=0, bytes_accessed=devices * rows * HEAD_DIM * 4
        ),
        compiler_params=pltpu.CompilerParams(vmem_limit_bytes=56 * MIB),
        name="pack_all",
    )(keys, values, queries)


def pack_rest_kernel(head_axis, start, each, first, count, peers, lists, counts, k_ref, v_ref, q_ref, *refs):
    outs, sem = refs[:peers], refs[peers]
    me, mine = lax.axis_index(head_axis), lax.axis_index("uly")
    copies = []
    for rel in range(peers):
        for part, src in enumerate((k_ref, v_ref, q_ref)):
            for i in range(count):
                col = pl.multiple_of((start + (me ^ rel) * each + first + i) * HEAD_DIM, HEAD_DIM)
                row = (part * count + i) * BLOCK_LEN + (part == 2) * TABLE_ROWS
                copies.append(
                    pltpu.make_async_copy(
                        src.at[:, pl.ds(col, HEAD_DIM)], outs[rel].at[pl.ds(row, BLOCK_LEN)], sem
                    )
                )
    for copy in copies:
        copy.start()
    lane = lax.broadcasted_iota(jnp.int32, (TABLE_ROWS, HEAD_DIM), 1)
    table = jnp.where(lane == LIST_LEN, counts[mine], 0)
    for e in range(LIST_LEN):
        table = jnp.where(lane == e, lists[mine, e], table)
    table = table.astype(jnp.float32).astype(jnp.bfloat16)
    for rel in range(peers):
        row = 2 * count * BLOCK_LEN
        outs[rel][row : row + TABLE_ROWS] = table
    for copy in copies:
        copy.wait()


def pack_rest(queries, keys, values, lists, counts, head_axis, start, each, first, count):
    peers = lax.axis_size(head_axis)
    rows = 3 * count * BLOCK_LEN + TABLE_ROWS
    return pl.pallas_call(
        functools.partial(pack_rest_kernel, head_axis, start, each, first, count, peers),
        out_shape=[jax.ShapeDtypeStruct((rows, HEAD_DIM), queries.dtype)] * peers,
        in_specs=[SMEM] * 2 + [ANY] * 3,
        out_specs=[pl.BlockSpec(memory_space=pltpu.VMEM)] * peers,
        scratch_shapes=[pltpu.SemaphoreType.DMA],
        cost_estimate=pl.CostEstimate(
            flops=0, transcendentals=0, bytes_accessed=peers * rows * HEAD_DIM * 4
        ),
        compiler_params=pltpu.CompilerParams(vmem_limit_bytes=56 * MIB),
        name="pack_rest",
    )(lists, counts, keys, values, queries)


def attend_blocks(queries, useds, pairs, write):
    most = functools.reduce(jnp.maximum, useds)

    def run(entries):
        scores, values = [], []
        for t, q in enumerate(queries):
            k, v = pairs(t, entries)
            s = []
            for e in range(0, entries, 2):
                both = lax.dot_general(
                    q,
                    jnp.concatenate(k[e : e + 2], axis=0),
                    (((1,), (1,)), ((), ())),
                    preferred_element_type=jnp.float32,
                )
                s += [both[:, :BLOCK_LEN], both[:, BLOCK_LEN:]]
            for e in range(MIN_COUNT, entries):
                s[e] = s[e] + jnp.where(useds[t] > e, 0.0, -jnp.inf).astype(jnp.float32)
            scores.append(s)
            values.append(v)
        for t, (s, v) in enumerate(zip(scores, values)):
            top = jnp.max(functools.reduce(jnp.maximum, s), axis=1, keepdims=True)
            w = [jnp.exp2((s_e - top) * SCORE_FACTOR) for s_e in s]
            total = jnp.sum(functools.reduce(jnp.add, w), axis=1, keepdims=True)
            blended = jnp.dot(
                jnp.concatenate([w_e.astype(jnp.bfloat16) for w_e in w], axis=1),
                jnp.concatenate(v, axis=0),
                preferred_element_type=jnp.float32,
            )
            write(t, (blended * (1.0 / total)).astype(jnp.bfloat16))

    for entries in range(MIN_COUNT, LIST_LEN + 1, 2):
        pl.when((most == entries) | (most == entries - 1))(functools.partial(run, entries))


def attend_all_kernel(full, place, table_ref, buf, out_ref, table, o_buf, in_sem, out_sem):
    devices = buf.shape[0]
    copy = pltpu.make_async_copy(table_ref, table, in_sem)
    copy.start()
    copy.wait()

    def step(j, carry):
        blocks = [table[devices * ROW + j * TOGETHER + t] for t in range(TOGETHER)]
        rows = [place(block) * ROW for block in blocks]
        useds = [table[row + LIST_LEN] for row in rows]
        for i in range(full):
            own = pl.ds(i * BLOCK_LEN, BLOCK_LEN)

            def pairs(t, entries):
                named = [table[rows[t] + e] for e in range(entries)]
                keys = [buf[b, own] for b in named]
                return keys, [buf[b, pl.ds((full + i) * BLOCK_LEN, BLOCK_LEN)] for b in named]

            def write(t, result):
                o_buf[blocks[t], own] = result

            queries = [buf[b, pl.ds((2 * full + i) * BLOCK_LEN, BLOCK_LEN)] for b in blocks]
            attend_blocks(queries, useds, pairs, write)
        for block in blocks:
            pltpu.make_async_copy(o_buf.at[block], out_ref.at[block], out_sem).start()
        return carry

    lax.fori_loop(0, devices // TOGETHER, step, 0)
    pltpu.make_async_copy(o_buf, out_ref, out_sem).wait()


def attend_cost(blocks, heads, in_bytes):
    pairs = blocks * heads * LIST_LEN
    return pl.CostEstimate(
        flops=pairs * 4 * BLOCK_LEN * BLOCK_LEN * HEAD_DIM,
        transcendentals=pairs * BLOCK_LEN * BLOCK_LEN,
        bytes_accessed=in_bytes,
    )


def attend_all(table, arrived, full, place):
    devices = arrived.shape[0]
    shape = (devices, full * BLOCK_LEN, HEAD_DIM)
    return pl.pallas_call(
        functools.partial(attend_all_kernel, full, place),
        out_shape=pltpu.HBM(shape, jnp.bfloat16),
        in_specs=[HBM, pl.BlockSpec(memory_space=pltpu.VMEM)],
        out_specs=HBM,
        scratch_shapes=[
            pltpu.SMEM(table.shape, jnp.int32),
            pltpu.VMEM(shape, jnp.bfloat16),
            pltpu.SemaphoreType.DMA,
            pltpu.SemaphoreType.DMA,
        ],
        compiler_params=pltpu.CompilerParams(vmem_limit_bytes=16 * MIB),
        cost_estimate=attend_cost(devices, full, arrived.size * 2),
        name="attend_all",
    )(table, arrived)


def by_count(counts, blocks):
    index = jnp.arange(counts.size, dtype=jnp.int32)
    key = counts * counts.size + index
    rank = jnp.sum((key[None, :] < key[:, None]).astype(jnp.int32), axis=1)
    return jnp.sum(jnp.where(rank[None, :] == index[:, None], blocks[None, :], 0), axis=1)


def block_ids(head_axis, gather_axis):
    index = jnp.arange(lax.axis_size(DEVICES), dtype=jnp.int32)
    peers = lax.axis_size(head_axis)
    head = (index % peers) ^ lax.axis_index(head_axis)
    other = (index // peers) ^ lax.axis_index(gather_axis)
    return head * lax.axis_size("uly") + other if head_axis == "seq" else other * lax.axis_size("uly") + head


def stack_kernel(peers, rows, *refs):
    pieces, (kv_ref, q_ref, sem) = refs[:peers], refs[peers:]
    copies = []
    for rel, piece in enumerate(pieces):
        copies.append(pltpu.make_async_copy(piece.at[pl.ds(0, rows)], kv_ref.at[rel], sem))
        rest = pl.ds(rows, piece.shape[0] - rows)
        copies.append(pltpu.make_async_copy(piece.at[rest], q_ref.at[rel], sem))
    for copy in copies:
        copy.start()
    for copy in copies:
        copy.wait()


def stack(pieces, rows):
    peers, rest = len(pieces), pieces[0].shape[0] - rows
    vmem = pl.BlockSpec(memory_space=pltpu.VMEM)
    return pl.pallas_call(
        functools.partial(stack_kernel, peers, rows),
        out_shape=[jax.ShapeDtypeStruct((peers, n, HEAD_DIM), jnp.bfloat16) for n in (rows, rest)],
        in_specs=[ANY] * peers,
        out_specs=[vmem] * 2,
        scratch_shapes=[pltpu.SemaphoreType.DMA],
        cost_estimate=pl.CostEstimate(
            flops=0, transcendentals=0, bytes_accessed=4 * peers * (rows + rest) * HEAD_DIM
        ),
        compiler_params=pltpu.CompilerParams(vmem_limit_bytes=12 * MIB),
        name="stack",
    )(*[pltpu.with_memory_space_constraint(piece, pltpu.HBM) for piece in pieces])


def attend_rest_kernel(head_axis, gather_axis, count, peers, others, place, table, *refs):
    q_ref, gathered, refs = refs[0], refs[1 : others + 1], refs[others + 1 :]
    outs, refs = refs[:peers], refs[peers:]
    q_buf, kv_buf, o_buf, in_sem, out_sem = refs
    part_rows = count * BLOCK_LEN
    copies = [pltpu.make_async_copy(q_ref, q_buf, in_sem)]
    copies += [
        pltpu.make_async_copy(part.at[:, pl.ds(0, 2 * part_rows)], kv_buf.at[pl.ds(g * peers, peers)], in_sem)
        for g, part in enumerate(gathered)
    ]
    for copy in copies:
        copy.start()
    for copy in copies:
        copy.wait()
    my_head, my_gather = lax.axis_index(head_axis), lax.axis_index(gather_axis)
    inner = lax.axis_size("uly")

    def step(j, carry):
        mine = [j * TOGETHER + t for t in range(TOGETHER)]
        heads = [my_head ^ rel for rel in mine]
        blocks = [h * inner + my_gather if head_axis == "seq" else my_gather * inner + h for h in heads]
        rows = [place(block) * ROW for block in blocks]
        useds = [table[row + LIST_LEN] for row in rows]
        for i in range(count):
            own = pl.ds(i * BLOCK_LEN, BLOCK_LEN)

            def pairs(t, entries):
                slots = [place(table[rows[t] + e]) for e in range(entries)]
                keys = [kv_buf[slot, own] for slot in slots]
                return keys, [kv_buf[slot, pl.ds((count + i) * BLOCK_LEN, BLOCK_LEN)] for slot in slots]

            def write(t, result):
                o_buf[mine[t], own] = result

            attend_blocks([q_buf[r, own] for r in mine], useds, pairs, write)
        return carry

    lax.fori_loop(0, peers // TOGETHER, step, 0)
    copies = [
        pltpu.make_async_copy(o_buf.at[rel], outs[rel], out_sem) for rel in range(peers)
    ]
    for copy in copies:
        copy.start()
    for copy in copies:
        copy.wait()


def attend_rest(table, queries, gathered, head_axis, gather_axis, count, place):
    peers, others = lax.axis_size(head_axis), lax.axis_size(gather_axis)
    part_rows = count * BLOCK_LEN
    kv_shape = (others * peers, 2 * part_rows, HEAD_DIM)
    return pl.pallas_call(
        functools.partial(attend_rest_kernel, head_axis, gather_axis, count, peers, others, place),
        out_shape=[jax.ShapeDtypeStruct((part_rows, HEAD_DIM), jnp.bfloat16)] * peers,
        in_specs=[SMEM] + [ANY] * (1 + others),
        out_specs=[ANY] * peers,
        scratch_shapes=[
            pltpu.VMEM((peers, part_rows, HEAD_DIM), jnp.bfloat16),
            pltpu.VMEM(kv_shape, jnp.bfloat16),
            pltpu.VMEM((peers, part_rows, HEAD_DIM), jnp.bfloat16),
            pltpu.SemaphoreType.DMA,
            pltpu.SemaphoreType.DMA,
        ],
        compiler_params=pltpu.CompilerParams(vmem_limit_bytes=2 * math.prod(kv_shape) + 8 * MIB),
        cost_estimate=attend_cost(peers, count, 2 * math.prod(kv_shape)),
        name="attend_rest",
    )(table, queries, *gathered)


def unpack_kernel(head_axis, start, each, full, chunks, peers, devices, *refs):
    has_main = 1 if full else 0
    n = has_main + len(chunks) * peers
    parts, out_ref, buf, in_sem, out_sem = refs[:n], refs[n], refs[n + 1], refs[n + 2], refs[n + 3]
    me = lax.axis_index(head_axis)
    copies = []
    for d in range(devices * has_main):
        for i in range(full):
            copies.append(
                pltpu.make_async_copy(
                    parts[0].at[d, pl.ds(i * BLOCK_LEN, BLOCK_LEN)],
                    buf.at[:, pl.ds((d * full + i) * HEAD_DIM, HEAD_DIM)],
                    in_sem,
                )
            )
    for j, (first, count) in enumerate(chunks):
        for rel in range(peers):
            for i in range(count):
                col = pl.multiple_of((start + (me ^ rel) * each + first + i) * HEAD_DIM, HEAD_DIM)
                copies.append(
                    pltpu.make_async_copy(
                        parts[has_main + j * peers + rel].at[pl.ds(i * BLOCK_LEN, BLOCK_LEN)],
                        buf.at[:, pl.ds(col, HEAD_DIM)],
                        in_sem,
                    )
                )
    for copy in copies:
        copy.start()
    for copy in copies:
        copy.wait()
    copy = pltpu.make_async_copy(buf, out_ref, out_sem)
    copy.start()
    copy.wait()


def unpack(parts, head_axis, start, each, full, chunks, devices, width):
    peers = lax.axis_size(head_axis)
    return pl.pallas_call(
        functools.partial(unpack_kernel, head_axis, start, each, full, chunks, peers, devices),
        out_shape=jax.ShapeDtypeStruct((BLOCK_LEN, width), jnp.bfloat16),
        in_specs=[ANY] * len(parts),
        out_specs=ANY,
        scratch_shapes=[
            pltpu.VMEM((BLOCK_LEN, width), jnp.bfloat16),
            pltpu.SemaphoreType.DMA,
            pltpu.SemaphoreType.DMA,
        ],
        cost_estimate=pl.CostEstimate(
            flops=0, transcendentals=0, bytes_accessed=2 * BLOCK_LEN * width * 2
        ),
        compiler_params=pltpu.CompilerParams(vmem_limit_bytes=8 * MIB),
        name="unpack",
    )(*parts)


def body(queries, keys, values, block_lists, block_counts):
    width = queries.shape[1]
    heads = width // HEAD_DIM
    devices = lax.axis_size(DEVICES)
    assert queries.shape[0] == BLOCK_LEN
    full = heads // devices
    start = full * devices
    head_axis, gather_axis = "seq", "uly"
    if (heads - start) % lax.axis_size(head_axis):
        head_axis, gather_axis = gather_axis, head_axis
    peers = lax.axis_size(head_axis)
    each = (heads - start) // peers
    chunks = tuple((first, min(CHUNK, each - first)) for first in range(0, each, CHUNK))
    half = peers // 2
    order = [rel for pair in zip(range(half, peers), [1, *range(2, half), 0]) for rel in pair if rel]
    place = functools.partial(row_of, head_axis=head_axis, gather_axis=gather_axis)
    assert devices <= 256

    arrivals, tied = [], []
    for first, count in chunks:
        sends = pack_rest(
            queries, keys, values, block_lists, block_counts, head_axis, start, each, first, count
        )
        queries, keys, values, sends = lax.optimization_barrier((queries, keys, values, sends))
        moved = {rel: swap(sends[rel], head_axis, rel) for rel in order}
        tied.extend(moved[rel] for rel in order[:TIED])
        arrivals.append([sends[0]] + [moved[rel] for rel in range(1, peers)])
    if full:
        sent = pack_all(queries, keys, values, full, devices)
        sent, _ = lax.optimization_barrier((sent, tied))
        arrived = lax.all_to_all(sent, DEVICES, split_axis=0, concat_axis=0, tiled=True)
    outputs, table = [], None
    for (first, count), pieces in zip(chunks, arrivals):
        kv_rows = 2 * count * BLOCK_LEN
        kv, q = stack(pieces, kv_rows + TABLE_ROWS)
        gathered = gather_all(kv, gather_axis)
        if table is None:
            table = jnp.concatenate([part[:, kv_rows, :ROW] for part in gathered])
            table = table.astype(jnp.int32)
            counts, table = table[:, LIST_LEN], table.reshape(-1)
        outputs.append(attend_rest(table, q, gathered, head_axis, gather_axis, count, place))
    results, backs = [], []
    if full:
        ordered = jnp.concatenate([table, by_count(counts, block_ids(head_axis, gather_axis))])
        arrived, ordered, _ = lax.optimization_barrier((arrived, ordered, outputs))
        blended = attend_all(ordered, arrived, full, place)
    for outs in outputs:
        late = list(range(half, peers)) + list(range(half - 1, 0, -1))
        moved = {rel: swap(outs[rel], head_axis, rel) for rel in late}
        if full:
            early = late[:IN_FLIGHT]
            blended, kept = lax.optimization_barrier((blended, [moved[rel] for rel in early]))
            moved.update(zip(early, kept))
        backs.extend([outs[0]] + [moved[rel] for rel in range(1, peers)])
    if full:
        results.append(lax.all_to_all(blended, DEVICES, split_axis=0, concat_axis=0, tiled=True))
    results.extend(backs)
    return unpack(results, head_axis, start, each, full, chunks, devices, width)


def solution(mesh):
    rows = P(DEVICES, None)
    placed = (rows, rows, rows, P("seq", None), P("seq"))
    return jax.shard_map(body, mesh=mesh, in_specs=placed, out_specs=rows, check_vma=False)
```

```python
import functools
import math

import jax
import jax.numpy as jnp
from jax import lax
from jax.experimental import pallas as pl
from jax.experimental.pallas import tpu as pltpu
from jax.sharding import PartitionSpec as P

HEAD_DIM = 128
BLOCK_LEN = 128
LIST_LEN = 12
MIN_COUNT = 4
ROW = LIST_LEN + 1
MIB = 1024 * 1024
CHUNK = 2
TOGETHER = 8
REST_TOGETHER = 4
TABLE_ROWS = 16
IN_FLIGHT = 5
TIED = 7
SCORE_FACTOR = HEAD_DIM**-0.5 * math.log2(math.e)
ANY = pl.BlockSpec(memory_space=pl.ANY)
SMEM = pl.BlockSpec(memory_space=pltpu.SMEM)
HBM = pl.BlockSpec(memory_space=pltpu.HBM)
DEVICES = ("seq", "uly")


def swap(x, axis, bit):
    return lax.ppermute(x, axis, [(i, i ^ bit) for i in range(lax.axis_size(axis))])


def gather_all(x, axis):
    parts, bit = {0: x}, 1
    while bit < lax.axis_size(axis):
        parts.update({rel | bit: swap(part, axis, bit) for rel, part in list(parts.items())})
        bit *= 2
    return [parts[rel] for rel in range(lax.axis_size(axis))]


def row_of(block, head_axis, gather_axis):
    inner = lax.axis_size("uly")
    outer, low = block // inner, block % inner
    head, other = (outer, low) if head_axis == "seq" else (low, outer)
    return (other ^ lax.axis_index(gather_axis)) * lax.axis_size(head_axis) + (
        head ^ lax.axis_index(head_axis)
    )


def pack_all_kernel(full, step, k_ref, v_ref, q_ref, out_ref):
    for d in range(step):
        for part, src in enumerate((k_ref, v_ref, q_ref)):
            for i in range(full):
                col = (d * full + i) * HEAD_DIM
                row = (part * full + i) * BLOCK_LEN
                out_ref[d, row : row + BLOCK_LEN] = src[:, col : col + HEAD_DIM]


def pack_all(queries, keys, values, full, devices):
    step = devices // 4
    block = pl.BlockSpec((BLOCK_LEN, step * full * HEAD_DIM), lambda j: (0, j))
    rows = 3 * full * BLOCK_LEN
    return pl.pallas_call(
        functools.partial(pack_all_kernel, full, step),
        grid=(devices // step,),
        out_shape=jax.ShapeDtypeStruct((devices, rows, HEAD_DIM), queries.dtype),
        in_specs=[block] * 3,
        out_specs=pl.BlockSpec((step, rows, HEAD_DIM), lambda j: (j, 0, 0)),
        cost_estimate=pl.CostEstimate(
            flops=0, transcendentals=0, bytes_accessed=devices * rows * HEAD_DIM * 4
        ),
        compiler_params=pltpu.CompilerParams(vmem_limit_bytes=56 * MIB),
        name="pack_all",
    )(keys, values, queries)


def pack_rest_kernel(head_axis, start, each, first, count, peers, lists, counts, k_ref, v_ref, q_ref, *refs):
    outs, sem = refs[:peers], refs[peers]
    me, mine = lax.axis_index(head_axis), lax.axis_index("uly")
    copies = []
    for rel in range(peers):
        for part, src in enumerate((k_ref, v_ref, q_ref)):
            for i in range(count):
                col = pl.multiple_of((start + (me ^ rel) * each + first + i) * HEAD_DIM, HEAD_DIM)
                row = (part * count + i) * BLOCK_LEN + (part == 2) * TABLE_ROWS
                copies.append(
                    pltpu.make_async_copy(
                        src.at[:, pl.ds(col, HEAD_DIM)], outs[rel].at[pl.ds(row, BLOCK_LEN)], sem
                    )
                )
    for copy in copies:
        copy.start()
    lane = lax.broadcasted_iota(jnp.int32, (TABLE_ROWS, HEAD_DIM), 1)
    table = jnp.where(lane == LIST_LEN, counts[mine], 0)
    for e in range(LIST_LEN):
        table = jnp.where(lane == e, lists[mine, e], table)
    table = table.astype(jnp.float32).astype(jnp.bfloat16)
    for rel in range(peers):
        row = 2 * count * BLOCK_LEN
        outs[rel][row : row + TABLE_ROWS] = table
    for copy in copies:
        copy.wait()


def pack_rest(queries, keys, values, lists, counts, head_axis, start, each, first, count):
    peers = lax.axis_size(head_axis)
    rows = 3 * count * BLOCK_LEN + TABLE_ROWS
    return pl.pallas_call(
        functools.partial(pack_rest_kernel, head_axis, start, each, first, count, peers),
        out_shape=[pltpu.VMEM((rows, HEAD_DIM), queries.dtype)] * peers,
        in_specs=[SMEM] * 2 + [ANY] * 3,
        out_specs=[pl.BlockSpec(memory_space=pltpu.VMEM)] * peers,
        scratch_shapes=[pltpu.SemaphoreType.DMA],
        cost_estimate=pl.CostEstimate(
            flops=0, transcendentals=0, bytes_accessed=peers * rows * HEAD_DIM * 4
        ),
        compiler_params=pltpu.CompilerParams(vmem_limit_bytes=60 * MIB),
        name="pack_rest",
    )(lists, counts, keys, values, queries)


def attend_blocks(queries, useds, pairs, write):
    most = functools.reduce(jnp.maximum, useds)

    def run(entries):
        scores, values = [], []
        for t, q in enumerate(queries):
            k, v = pairs(t, entries)
            s = []
            for e in range(0, entries, 2):
                both = lax.dot_general(
                    q,
                    jnp.concatenate(k[e : e + 2], axis=0),
                    (((1,), (1,)), ((), ())),
                    preferred_element_type=jnp.float32,
                )
                s += [both[:, :BLOCK_LEN], both[:, BLOCK_LEN:]]
            for e in range(MIN_COUNT, entries):
                s[e] = s[e] + jnp.where(useds[t] > e, 0.0, -jnp.inf).astype(jnp.float32)
            scores.append(s)
            values.append(v)
        for t, (s, v) in enumerate(zip(scores, values)):
            top = jnp.max(functools.reduce(jnp.maximum, s), axis=1, keepdims=True)
            w = [jnp.exp2((s_e - top) * SCORE_FACTOR) for s_e in s]
            total = jnp.sum(functools.reduce(jnp.add, w), axis=1, keepdims=True)
            blended = jnp.dot(
                jnp.concatenate([w_e.astype(jnp.bfloat16) for w_e in w], axis=1),
                jnp.concatenate(v, axis=0),
                preferred_element_type=jnp.float32,
            )
            write(t, (blended * (1.0 / total)).astype(jnp.bfloat16))

    for entries in range(MIN_COUNT, LIST_LEN + 1, 2):
        pl.when((most == entries) | (most == entries - 1))(functools.partial(run, entries))


def attend_all_kernel(full, place, table_ref, buf, out_ref, table, o_buf, in_sem, out_sem):
    devices = buf.shape[0]
    copy = pltpu.make_async_copy(table_ref, table, in_sem)
    copy.start()
    copy.wait()

    def step(j, carry):
        blocks = [table[devices * ROW + j * TOGETHER + t] for t in range(TOGETHER)]
        rows = [place(block) * ROW for block in blocks]
        useds = [table[row + LIST_LEN] for row in rows]
        for i in range(full):
            own = pl.ds(i * BLOCK_LEN, BLOCK_LEN)

            def pairs(t, entries):
                named = [table[rows[t] + e] for e in range(entries)]
                keys = [buf[b, own] for b in named]
                return keys, [buf[b, pl.ds((full + i) * BLOCK_LEN, BLOCK_LEN)] for b in named]

            def write(t, result):
                o_buf[blocks[t], own] = result

            queries = [buf[b, pl.ds((2 * full + i) * BLOCK_LEN, BLOCK_LEN)] for b in blocks]
            attend_blocks(queries, useds, pairs, write)
        for block in blocks:
            pltpu.make_async_copy(o_buf.at[block], out_ref.at[block], out_sem).start()
        return carry

    lax.fori_loop(0, devices // TOGETHER, step, 0)
    pltpu.make_async_copy(o_buf, out_ref, out_sem).wait()


def attend_cost(blocks, heads, in_bytes):
    pairs = blocks * heads * LIST_LEN
    return pl.CostEstimate(
        flops=pairs * 4 * BLOCK_LEN * BLOCK_LEN * HEAD_DIM,
        transcendentals=pairs * BLOCK_LEN * BLOCK_LEN,
        bytes_accessed=in_bytes,
    )


def attend_all(table, arrived, full, place):
    devices = arrived.shape[0]
    shape = (devices, full * BLOCK_LEN, HEAD_DIM)
    return pl.pallas_call(
        functools.partial(attend_all_kernel, full, place),
        out_shape=pltpu.HBM(shape, jnp.bfloat16),
        in_specs=[HBM, pl.BlockSpec(memory_space=pltpu.VMEM)],
        out_specs=HBM,
        scratch_shapes=[
            pltpu.SMEM(table.shape, jnp.int32),
            pltpu.VMEM(shape, jnp.bfloat16),
            pltpu.SemaphoreType.DMA,
            pltpu.SemaphoreType.DMA,
        ],
        compiler_params=pltpu.CompilerParams(vmem_limit_bytes=16 * MIB),
        cost_estimate=attend_cost(devices, full, arrived.size * 2),
        name="attend_all",
    )(table, arrived)


def by_count(counts, blocks):
    index = jnp.arange(counts.size, dtype=jnp.int32)
    key = counts * counts.size + index
    rank = jnp.sum((key[None, :] < key[:, None]).astype(jnp.int32), axis=1)
    return jnp.sum(jnp.where(rank[None, :] == index[:, None], blocks[None, :], 0), axis=1)


def block_ids(head_axis, gather_axis):
    index = jnp.arange(lax.axis_size(DEVICES), dtype=jnp.int32)
    peers = lax.axis_size(head_axis)
    head = (index % peers) ^ lax.axis_index(head_axis)
    other = (index // peers) ^ lax.axis_index(gather_axis)
    return head * lax.axis_size("uly") + other if head_axis == "seq" else other * lax.axis_size("uly") + head


def stack_kernel(peers, rows, *refs):
    pieces, (kv_ref, q_ref, sem) = refs[:peers], refs[peers:]
    copies = []
    for rel, piece in enumerate(pieces):
        copies.append(pltpu.make_async_copy(piece.at[pl.ds(0, rows)], kv_ref.at[rel], sem))
        rest = pl.ds(rows, piece.shape[0] - rows)
        copies.append(pltpu.make_async_copy(piece.at[rest], q_ref.at[rel], sem))
    for copy in copies:
        copy.start()
    for copy in copies:
        copy.wait()


def stack(pieces, rows):
    peers, rest = len(pieces), pieces[0].shape[0] - rows
    vmem = pl.BlockSpec(memory_space=pltpu.VMEM)
    return pl.pallas_call(
        functools.partial(stack_kernel, peers, rows),
        out_shape=[jax.ShapeDtypeStruct((peers, n, HEAD_DIM), jnp.bfloat16) for n in (rows, rest)],
        in_specs=[ANY] * peers,
        out_specs=[vmem] * 2,
        scratch_shapes=[pltpu.SemaphoreType.DMA],
        cost_estimate=pl.CostEstimate(
            flops=0, transcendentals=0, bytes_accessed=4 * peers * (rows + rest) * HEAD_DIM
        ),
        compiler_params=pltpu.CompilerParams(vmem_limit_bytes=12 * MIB),
        name="stack",
    )(pieces[0], *[pltpu.with_memory_space_constraint(piece, pltpu.HBM) for piece in pieces[1:]])


def attend_rest_kernel(head_axis, gather_axis, count, peers, others, place, table, *refs):
    q_ref, gathered, refs = refs[0], refs[1 : others + 1], refs[others + 1 :]
    outs, refs = refs[:peers], refs[peers:]
    q_buf, kv_buf, o_buf, in_sem, out_sem = refs
    part_rows = count * BLOCK_LEN
    copies = [pltpu.make_async_copy(q_ref, q_buf, in_sem)]
    copies += [
        pltpu.make_async_copy(part.at[:, pl.ds(0, 2 * part_rows)], kv_buf.at[pl.ds(g * peers, peers)], in_sem)
        for g, part in enumerate(gathered)
    ]
    for copy in copies:
        copy.start()
    for copy in copies:
        copy.wait()
    def step(j, carry):
        mine = [j * REST_TOGETHER + t for t in range(REST_TOGETHER)]
        rows = [rel * ROW for rel in mine]
        useds = [table[row + LIST_LEN] for row in rows]
        for i in range(count):
            own = pl.ds(i * BLOCK_LEN, BLOCK_LEN)

            def pairs(t, entries):
                slots = [place(table[rows[t] + e]) for e in range(entries)]
                keys = [kv_buf[slot, own] for slot in slots]
                return keys, [kv_buf[slot, pl.ds((count + i) * BLOCK_LEN, BLOCK_LEN)] for slot in slots]

            def write(t, result):
                o_buf[mine[t], own] = result

            attend_blocks([q_buf[r, own] for r in mine], useds, pairs, write)
        return carry

    lax.fori_loop(0, peers // REST_TOGETHER, step, 0)
    copies = [
        pltpu.make_async_copy(o_buf.at[rel], outs[rel], out_sem) for rel in range(peers)
    ]
    for copy in copies:
        copy.start()
    for copy in copies:
        copy.wait()


def attend_rest(table, queries, gathered, head_axis, gather_axis, count, place):
    peers, others = lax.axis_size(head_axis), lax.axis_size(gather_axis)
    part_rows = count * BLOCK_LEN
    kv_shape = (others * peers, 2 * part_rows, HEAD_DIM)
    return pl.pallas_call(
        functools.partial(attend_rest_kernel, head_axis, gather_axis, count, peers, others, place),
        out_shape=[jax.ShapeDtypeStruct((part_rows, HEAD_DIM), jnp.bfloat16)] * peers,
        in_specs=[SMEM] + [ANY] * (1 + others),
        out_specs=[ANY] * peers,
        scratch_shapes=[
            pltpu.VMEM((peers, part_rows, HEAD_DIM), jnp.bfloat16),
            pltpu.VMEM(kv_shape, jnp.bfloat16),
            pltpu.VMEM((peers, part_rows, HEAD_DIM), jnp.bfloat16),
            pltpu.SemaphoreType.DMA,
            pltpu.SemaphoreType.DMA,
        ],
        compiler_params=pltpu.CompilerParams(vmem_limit_bytes=2 * math.prod(kv_shape) + 8 * MIB),
        cost_estimate=attend_cost(peers, count, 2 * math.prod(kv_shape)),
        name="attend_rest",
    )(table, pltpu.with_memory_space_constraint(queries, pltpu.HBM), *gathered)


def unpack_kernel(head_axis, start, each, full, chunks, peers, devices, *refs):
    has_main = 1 if full else 0
    n = has_main + len(chunks) * peers
    parts, out_ref, sem = refs[:n], refs[n], refs[n + 1]
    me = lax.axis_index(head_axis)
    copies = []
    for d in range(devices * has_main):
        for i in range(full):
            copies.append(
                pltpu.make_async_copy(
                    parts[0].at[d, pl.ds(i * BLOCK_LEN, BLOCK_LEN)],
                    out_ref.at[:, pl.ds((d * full + i) * HEAD_DIM, HEAD_DIM)],
                    sem,
                )
            )
    for j, (first, count) in enumerate(chunks):
        for rel in range(peers):
            for i in range(count):
                col = pl.multiple_of((start + (me ^ rel) * each + first + i) * HEAD_DIM, HEAD_DIM)
                copies.append(
                    pltpu.make_async_copy(
                        parts[has_main + j * peers + rel].at[pl.ds(i * BLOCK_LEN, BLOCK_LEN)],
                        out_ref.at[:, pl.ds(col, HEAD_DIM)],
                        sem,
                    )
                )
    for copy in copies:
        copy.start()
    for copy in copies:
        copy.wait()


def unpack(parts, head_axis, start, each, full, chunks, devices, width):
    peers = lax.axis_size(head_axis)
    return pl.pallas_call(
        functools.partial(unpack_kernel, head_axis, start, each, full, chunks, peers, devices),
        out_shape=jax.ShapeDtypeStruct((BLOCK_LEN, width), jnp.bfloat16),
        in_specs=[ANY] * len(parts),
        out_specs=ANY,
        scratch_shapes=[pltpu.SemaphoreType.DMA],
        cost_estimate=pl.CostEstimate(
            flops=0, transcendentals=0, bytes_accessed=2 * BLOCK_LEN * width * 2
        ),
        compiler_params=pltpu.CompilerParams(vmem_limit_bytes=8 * MIB),
        name="unpack",
    )(*parts)


def body(queries, keys, values, block_lists, block_counts):
    width = queries.shape[1]
    heads = width // HEAD_DIM
    devices = lax.axis_size(DEVICES)
    assert queries.shape[0] == BLOCK_LEN
    full = heads // devices
    start = full * devices
    head_axis, gather_axis = "seq", "uly"
    if (heads - start) % lax.axis_size(head_axis):
        head_axis, gather_axis = gather_axis, head_axis
    peers = lax.axis_size(head_axis)
    each = (heads - start) // peers
    chunks = tuple((first, min(CHUNK, each - first)) for first in range(0, each, CHUNK))
    half = peers // 2
    order = [rel for pair in zip(range(half, peers), [1, *range(2, half), 0]) for rel in pair if rel]
    place = functools.partial(row_of, head_axis=head_axis, gather_axis=gather_axis)
    assert devices <= 256

    arrivals, tied = [], []
    for first, count in chunks:
        sends = pack_rest(
            queries, keys, values, block_lists, block_counts, head_axis, start, each, first, count
        )
        queries, keys, values, sends = lax.optimization_barrier((queries, keys, values, sends))
        moved = {rel: swap(sends[rel], head_axis, rel) for rel in order}
        tied.extend(moved[rel] for rel in order[:TIED])
        arrivals.append([sends[0]] + [moved[rel] for rel in range(1, peers)])
    if full:
        sent = pack_all(queries, keys, values, full, devices)
        sent, _ = lax.optimization_barrier((sent, tied))
        arrived = lax.all_to_all(sent, DEVICES, split_axis=0, concat_axis=0, tiled=True)
    outputs, table = [], None
    for (first, count), pieces in zip(chunks, arrivals):
        kv_rows = 2 * count * BLOCK_LEN
        kv, q = stack(pieces, kv_rows + TABLE_ROWS)
        lists = kv[:, kv_rows, :ROW].astype(jnp.int32).reshape(-1)
        gathered = gather_all(kv, gather_axis)
        if table is None:
            table = jnp.concatenate([part[:, kv_rows, :ROW] for part in gathered]).astype(jnp.int32)
        outputs.append(attend_rest(lists, q, gathered, head_axis, gather_axis, count, place))
    results, backs = [], []
    if full:
        ordered = by_count(table[:, LIST_LEN], block_ids(head_axis, gather_axis))
        ordered = jnp.concatenate([table.reshape(-1), ordered])
        arrived, ordered, _ = lax.optimization_barrier((arrived, ordered, outputs))
        blended = attend_all(ordered, arrived, full, place)
    for outs in outputs:
        late = list(range(half, peers)) + list(range(half - 1, 0, -1))
        moved = {rel: swap(outs[rel], head_axis, rel) for rel in late}
        if full:
            early = late[:IN_FLIGHT]
            blended, kept = lax.optimization_barrier((blended, [moved[rel] for rel in early]))
            moved.update(zip(early, kept))
        backs.extend([outs[0]] + [moved[rel] for rel in range(1, peers)])
    if full:
        results.append(lax.all_to_all(blended, DEVICES, split_axis=0, concat_axis=0, tiled=True))
    results.extend(backs)
    return unpack(results, head_axis, start, each, full, chunks, devices, width)


def solution(mesh):
    rows = P(DEVICES, None)
    placed = (rows, rows, rows, P("seq", None), P("seq"))
    return jax.shard_map(body, mesh=mesh, in_specs=placed, out_specs=rows, check_vma=False)
```

```python
import functools
import math

import jax
import jax.numpy as jnp
from jax import lax
from jax.experimental import pallas as pl
from jax.experimental.pallas import tpu as pltpu
from jax.sharding import PartitionSpec as P

HEAD_DIM = 128
BLOCK_LEN = 128
LIST_LEN = 12
MIN_COUNT = 4
ROW = LIST_LEN + 1
MIB = 1024 * 1024
CHUNK = 2
TOGETHER = 8
REST_TOGETHER = 4
TABLE_ROWS = 16
IN_FLIGHT = 4
TIED = 7
SCORE_FACTOR = HEAD_DIM**-0.5 * math.log2(math.e)
ANY = pl.BlockSpec(memory_space=pl.ANY)
SMEM = pl.BlockSpec(memory_space=pltpu.SMEM)
HBM = pl.BlockSpec(memory_space=pltpu.HBM)
DEVICES = ("seq", "uly")


def swap(x, axis, bit):
    return lax.ppermute(x, axis, [(i, i ^ bit) for i in range(lax.axis_size(axis))])


def gather_all(x, axis):
    parts, bit = {0: x}, 1
    while bit < lax.axis_size(axis):
        parts.update({rel | bit: swap(part, axis, bit) for rel, part in list(parts.items())})
        bit *= 2
    return [parts[rel] for rel in range(lax.axis_size(axis))]


def row_of(block, head_axis, gather_axis):
    inner = lax.axis_size("uly")
    outer, low = block // inner, block % inner
    head, other = (outer, low) if head_axis == "seq" else (low, outer)
    return (other ^ lax.axis_index(gather_axis)) * lax.axis_size(head_axis) + (
        head ^ lax.axis_index(head_axis)
    )


def pack_all_kernel(full, step, k_ref, v_ref, q_ref, out_ref):
    for d in range(step):
        for part, src in enumerate((k_ref, v_ref, q_ref)):
            for i in range(full):
                col = (d * full + i) * HEAD_DIM
                row = (part * full + i) * BLOCK_LEN
                out_ref[d, row : row + BLOCK_LEN] = src[:, col : col + HEAD_DIM]


def pack_all(queries, keys, values, full, devices):
    step = devices // 4
    block = pl.BlockSpec((BLOCK_LEN, step * full * HEAD_DIM), lambda j: (0, j))
    rows = 3 * full * BLOCK_LEN
    return pl.pallas_call(
        functools.partial(pack_all_kernel, full, step),
        grid=(devices // step,),
        out_shape=jax.ShapeDtypeStruct((devices, rows, HEAD_DIM), queries.dtype),
        in_specs=[block] * 3,
        out_specs=pl.BlockSpec((step, rows, HEAD_DIM), lambda j: (j, 0, 0)),
        cost_estimate=pl.CostEstimate(
            flops=0, transcendentals=0, bytes_accessed=devices * rows * HEAD_DIM * 4
        ),
        compiler_params=pltpu.CompilerParams(vmem_limit_bytes=56 * MIB),
        name="pack_all",
    )(keys, values, queries)


def pack_rest_kernel(head_axis, start, each, first, count, peers, lists, counts, k_ref, v_ref, q_ref, *refs):
    outs, sem = refs[:peers], refs[peers]
    me, mine = lax.axis_index(head_axis), lax.axis_index("uly")
    copies = []
    for rel in range(peers):
        for part, src in enumerate((k_ref, v_ref, q_ref)):
            for i in range(count):
                col = pl.multiple_of((start + (me ^ rel) * each + first + i) * HEAD_DIM, HEAD_DIM)
                row = (part * count + i) * BLOCK_LEN + (part == 2) * TABLE_ROWS
                copies.append(
                    pltpu.make_async_copy(
                        src.at[:, pl.ds(col, HEAD_DIM)], outs[rel].at[pl.ds(row, BLOCK_LEN)], sem
                    )
                )
    for copy in copies:
        copy.start()
    lane = lax.broadcasted_iota(jnp.int32, (TABLE_ROWS, HEAD_DIM), 1)
    table = jnp.where(lane == LIST_LEN, counts[mine], 0)
    for e in range(LIST_LEN):
        table = jnp.where(lane == e, lists[mine, e], table)
    table = table.astype(jnp.float32).astype(jnp.bfloat16)
    for rel in range(peers):
        row = 2 * count * BLOCK_LEN
        outs[rel][row : row + TABLE_ROWS] = table
    for copy in copies:
        copy.wait()


def pack_rest(queries, keys, values, lists, counts, head_axis, start, each, first, count):
    peers = lax.axis_size(head_axis)
    rows = 3 * count * BLOCK_LEN + TABLE_ROWS
    return pl.pallas_call(
        functools.partial(pack_rest_kernel, head_axis, start, each, first, count, peers),
        out_shape=[pltpu.VMEM((rows, HEAD_DIM), queries.dtype)] * peers,
        in_specs=[SMEM] * 2 + [ANY] * 3,
        out_specs=[pl.BlockSpec(memory_space=pltpu.VMEM)] * peers,
        scratch_shapes=[pltpu.SemaphoreType.DMA],
        cost_estimate=pl.CostEstimate(
            flops=0, transcendentals=0, bytes_accessed=peers * rows * HEAD_DIM * 4
        ),
        compiler_params=pltpu.CompilerParams(vmem_limit_bytes=60 * MIB),
        name="pack_rest",
    )(lists, counts, keys, values, queries)


def attend_blocks(queries, useds, pairs, write):
    most = functools.reduce(jnp.maximum, useds)

    def run(entries):
        scores, values = [], []
        for t, q in enumerate(queries):
            k, v = pairs(t, entries)
            s = []
            for e in range(0, entries, 2):
                both = lax.dot_general(
                    q,
                    jnp.concatenate(k[e : e + 2], axis=0),
                    (((1,), (1,)), ((), ())),
                    preferred_element_type=jnp.float32,
                )
                s += [both[:, :BLOCK_LEN], both[:, BLOCK_LEN:]]
            for e in range(MIN_COUNT, entries):
                s[e] = s[e] + jnp.where(useds[t] > e, 0.0, -jnp.inf).astype(jnp.float32)
            scores.append(s)
            values.append(v)
        for t, (s, v) in enumerate(zip(scores, values)):
            top = jnp.max(functools.reduce(jnp.maximum, s), axis=1, keepdims=True)
            w = [jnp.exp2((s_e - top) * SCORE_FACTOR) for s_e in s]
            total = jnp.sum(functools.reduce(jnp.add, w), axis=1, keepdims=True)
            blended = jnp.dot(
                jnp.concatenate([w_e.astype(jnp.bfloat16) for w_e in w], axis=1),
                jnp.concatenate(v, axis=0),
                preferred_element_type=jnp.float32,
            )
            write(t, (blended * (1.0 / total)).astype(jnp.bfloat16))

    for entries in range(MIN_COUNT, LIST_LEN + 1, 2):
        pl.when((most == entries) | (most == entries - 1))(functools.partial(run, entries))


def attend_all_kernel(full, place, table, buf, out_ref, o_buf, out_sem):
    devices = buf.shape[0]

    def step(j, carry):
        blocks = [table[devices * ROW + j * TOGETHER + t] for t in range(TOGETHER)]
        rows = [place(block) * ROW for block in blocks]
        useds = [table[row + LIST_LEN] for row in rows]
        for i in range(full):
            own = pl.ds(i * BLOCK_LEN, BLOCK_LEN)

            def pairs(t, entries):
                named = [table[rows[t] + e] for e in range(entries)]
                keys = [buf[b, own] for b in named]
                return keys, [buf[b, pl.ds((full + i) * BLOCK_LEN, BLOCK_LEN)] for b in named]

            def write(t, result):
                o_buf[blocks[t], own] = result

            queries = [buf[b, pl.ds((2 * full + i) * BLOCK_LEN, BLOCK_LEN)] for b in blocks]
            attend_blocks(queries, useds, pairs, write)
        for block in blocks:
            pltpu.make_async_copy(o_buf.at[block], out_ref.at[block], out_sem).start()
        return carry

    lax.fori_loop(0, devices // TOGETHER, step, 0)
    pltpu.make_async_copy(o_buf, out_ref, out_sem).wait()


def attend_cost(blocks, heads, in_bytes):
    pairs = blocks * heads * LIST_LEN
    return pl.CostEstimate(
        flops=pairs * 4 * BLOCK_LEN * BLOCK_LEN * HEAD_DIM,
        transcendentals=pairs * BLOCK_LEN * BLOCK_LEN,
        bytes_accessed=in_bytes,
    )


def attend_all(table, arrived, full, place):
    devices = arrived.shape[0]
    shape = (devices, full * BLOCK_LEN, HEAD_DIM)
    return pl.pallas_call(
        functools.partial(attend_all_kernel, full, place),
        out_shape=pltpu.HBM(shape, jnp.bfloat16),
        in_specs=[SMEM, pl.BlockSpec(memory_space=pltpu.VMEM)],
        out_specs=HBM,
        scratch_shapes=[
            pltpu.VMEM(shape, jnp.bfloat16),
            pltpu.SemaphoreType.DMA,
        ],
        compiler_params=pltpu.CompilerParams(vmem_limit_bytes=16 * MIB),
        cost_estimate=attend_cost(devices, full, arrived.size * 2),
        name="attend_all",
    )(pltpu.with_memory_space_constraint(table, pltpu.SMEM), arrived)


def by_count(counts, blocks):
    index = jnp.arange(counts.size, dtype=jnp.int32)
    key = counts * counts.size + index
    rank = jnp.sum((key[None, :] < key[:, None]).astype(jnp.int32), axis=1)
    return jnp.sum(jnp.where(rank[None, :] == index[:, None], blocks[None, :], 0), axis=1)


def block_ids(head_axis, gather_axis):
    index = jnp.arange(lax.axis_size(DEVICES), dtype=jnp.int32)
    peers = lax.axis_size(head_axis)
    head = (index % peers) ^ lax.axis_index(head_axis)
    other = (index // peers) ^ lax.axis_index(gather_axis)
    return head * lax.axis_size("uly") + other if head_axis == "seq" else other * lax.axis_size("uly") + head


def stack_kernel(peers, rows, *refs):
    pieces, (kv_ref, q_ref, sem) = refs[:peers], refs[peers:]
    copies = []
    for rel, piece in enumerate(pieces):
        copies.append(pltpu.make_async_copy(piece.at[pl.ds(0, rows)], kv_ref.at[rel], sem))
        rest = pl.ds(rows, piece.shape[0] - rows)
        copies.append(pltpu.make_async_copy(piece.at[rest], q_ref.at[rel], sem))
    for copy in copies:
        copy.start()
    for copy in copies:
        copy.wait()


def stack(pieces, rows):
    peers, rest = len(pieces), pieces[0].shape[0] - rows
    vmem = pl.BlockSpec(memory_space=pltpu.VMEM)
    return pl.pallas_call(
        functools.partial(stack_kernel, peers, rows),
        out_shape=[jax.ShapeDtypeStruct((peers, n, HEAD_DIM), jnp.bfloat16) for n in (rows, rest)],
        in_specs=[ANY] * peers,
        out_specs=[vmem] * 2,
        scratch_shapes=[pltpu.SemaphoreType.DMA],
        cost_estimate=pl.CostEstimate(
            flops=0, transcendentals=0, bytes_accessed=4 * peers * (rows + rest) * HEAD_DIM
        ),
        compiler_params=pltpu.CompilerParams(vmem_limit_bytes=12 * MIB),
        name="stack",
    )(pieces[0], *[pltpu.with_memory_space_constraint(piece, pltpu.HBM) for piece in pieces[1:]])


def attend_rest_kernel(head_axis, gather_axis, count, peers, others, place, table, *refs):
    q_ref, gathered, refs = refs[0], refs[1 : others + 1], refs[others + 1 :]
    outs, refs = refs[:peers], refs[peers:]
    q_buf, kv_buf, o_buf, in_sem, out_sem = refs
    part_rows = count * BLOCK_LEN
    copies = [pltpu.make_async_copy(q_ref, q_buf, in_sem)]
    copies += [
        pltpu.make_async_copy(part.at[:, pl.ds(0, 2 * part_rows)], kv_buf.at[pl.ds(g * peers, peers)], in_sem)
        for g, part in enumerate(gathered)
    ]
    for copy in copies:
        copy.start()
    for copy in copies:
        copy.wait()
    def step(j, carry):
        mine = [j * REST_TOGETHER + t for t in range(REST_TOGETHER)]
        rows = [rel * ROW for rel in mine]
        useds = [table[row + LIST_LEN] for row in rows]
        for i in range(count):
            own = pl.ds(i * BLOCK_LEN, BLOCK_LEN)

            def pairs(t, entries):
                slots = [place(table[rows[t] + e]) for e in range(entries)]
                keys = [kv_buf[slot, own] for slot in slots]
                return keys, [kv_buf[slot, pl.ds((count + i) * BLOCK_LEN, BLOCK_LEN)] for slot in slots]

            def write(t, result):
                o_buf[mine[t], own] = result

            attend_blocks([q_buf[r, own] for r in mine], useds, pairs, write)
        return carry

    lax.fori_loop(0, peers // REST_TOGETHER, step, 0)
    copies = [
        pltpu.make_async_copy(o_buf.at[rel], outs[rel], out_sem) for rel in range(peers)
    ]
    for copy in copies:
        copy.start()
    for copy in copies:
        copy.wait()


def attend_rest(table, queries, gathered, head_axis, gather_axis, count, place):
    peers, others = lax.axis_size(head_axis), lax.axis_size(gather_axis)
    part_rows = count * BLOCK_LEN
    kv_shape = (others * peers, 2 * part_rows, HEAD_DIM)
    return pl.pallas_call(
        functools.partial(attend_rest_kernel, head_axis, gather_axis, count, peers, others, place),
        out_shape=[jax.ShapeDtypeStruct((part_rows, HEAD_DIM), jnp.bfloat16)] * peers,
        in_specs=[SMEM] + [ANY] * (1 + others),
        out_specs=[ANY] * peers,
        scratch_shapes=[
            pltpu.VMEM((peers, part_rows, HEAD_DIM), jnp.bfloat16),
            pltpu.VMEM(kv_shape, jnp.bfloat16),
            pltpu.VMEM((peers, part_rows, HEAD_DIM), jnp.bfloat16),
            pltpu.SemaphoreType.DMA,
            pltpu.SemaphoreType.DMA,
        ],
        compiler_params=pltpu.CompilerParams(vmem_limit_bytes=2 * math.prod(kv_shape) + 8 * MIB),
        cost_estimate=attend_cost(peers, count, 2 * math.prod(kv_shape)),
        name="attend_rest",
    )(table, pltpu.with_memory_space_constraint(queries, pltpu.HBM), *gathered)


def unpack_kernel(head_axis, start, each, full, chunks, peers, devices, *refs):
    has_main = 1 if full else 0
    n = has_main + len(chunks) * peers
    parts, out_ref, sem = refs[:n], refs[n], refs[n + 1]
    me = lax.axis_index(head_axis)
    copies = []
    for d in range(devices * has_main):
        for i in range(full):
            copies.append(
                pltpu.make_async_copy(
                    parts[0].at[d, pl.ds(i * BLOCK_LEN, BLOCK_LEN)],
                    out_ref.at[:, pl.ds((d * full + i) * HEAD_DIM, HEAD_DIM)],
                    sem,
                )
            )
    for j, (first, count) in enumerate(chunks):
        for rel in range(peers):
            for i in range(count):
                col = pl.multiple_of((start + (me ^ rel) * each + first + i) * HEAD_DIM, HEAD_DIM)
                copies.append(
                    pltpu.make_async_copy(
                        parts[has_main + j * peers + rel].at[pl.ds(i * BLOCK_LEN, BLOCK_LEN)],
                        out_ref.at[:, pl.ds(col, HEAD_DIM)],
                        sem,
                    )
                )
    for copy in copies:
        copy.start()
    for copy in copies:
        copy.wait()


def unpack(parts, head_axis, start, each, full, chunks, devices, width):
    peers = lax.axis_size(head_axis)
    return pl.pallas_call(
        functools.partial(unpack_kernel, head_axis, start, each, full, chunks, peers, devices),
        out_shape=jax.ShapeDtypeStruct((BLOCK_LEN, width), jnp.bfloat16),
        in_specs=[ANY] * len(parts),
        out_specs=ANY,
        scratch_shapes=[pltpu.SemaphoreType.DMA],
        cost_estimate=pl.CostEstimate(
            flops=0, transcendentals=0, bytes_accessed=2 * BLOCK_LEN * width * 2
        ),
        compiler_params=pltpu.CompilerParams(vmem_limit_bytes=8 * MIB),
        name="unpack",
    )(*parts)


def body(queries, keys, values, block_lists, block_counts):
    width = queries.shape[1]
    heads = width // HEAD_DIM
    devices = lax.axis_size(DEVICES)
    assert queries.shape[0] == BLOCK_LEN
    full = heads // devices
    start = full * devices
    head_axis, gather_axis = "seq", "uly"
    if (heads - start) % lax.axis_size(head_axis):
        head_axis, gather_axis = gather_axis, head_axis
    peers = lax.axis_size(head_axis)
    each = (heads - start) // peers
    chunks = tuple((first, min(CHUNK, each - first)) for first in range(0, each, CHUNK))
    half = peers // 2
    order = [rel for pair in zip(range(half, peers), [1, *range(2, half), 0]) for rel in pair if rel]
    place = functools.partial(row_of, head_axis=head_axis, gather_axis=gather_axis)
    assert devices <= 256

    arrivals, tied = [], []
    for first, count in chunks:
        sends = pack_rest(
            queries, keys, values, block_lists, block_counts, head_axis, start, each, first, count
        )
        queries, keys, values, sends = lax.optimization_barrier((queries, keys, values, sends))
        moved = {rel: swap(sends[rel], head_axis, rel) for rel in order}
        tied.extend(moved[rel] for rel in order[:TIED])
        arrivals.append([sends[0]] + [moved[rel] for rel in range(1, peers)])
    if full:
        sent = pack_all(queries, keys, values, full, devices)
        sent, _ = lax.optimization_barrier((sent, tied))
        arrived = lax.all_to_all(sent, DEVICES, split_axis=0, concat_axis=0, tiled=True)
    outputs, table = [], None
    for (first, count), pieces in zip(chunks, arrivals):
        kv_rows = 2 * count * BLOCK_LEN
        kv, q = stack(pieces, kv_rows + TABLE_ROWS)
        lists = kv[:, kv_rows, :ROW].astype(jnp.int32).reshape(-1)
        gathered = gather_all(kv, gather_axis)
        if table is None:
            table = jnp.concatenate([part[:, kv_rows, :ROW] for part in gathered]).astype(jnp.int32)
        outputs.append(attend_rest(lists, q, gathered, head_axis, gather_axis, count, place))
    results, backs = [], []
    if full:
        ordered = by_count(table[:, LIST_LEN], block_ids(head_axis, gather_axis))
        ordered = jnp.concatenate([table.reshape(-1), ordered])
        arrived, ordered, _ = lax.optimization_barrier((arrived, ordered, outputs))
        blended = attend_all(ordered, arrived, full, place)
    for outs in outputs:
        late = list(range(half, peers)) + list(range(half - 1, 0, -1))
        moved = {rel: swap(outs[rel], head_axis, rel) for rel in late}
        if full:
            early = late[:IN_FLIGHT]
            blended, kept = lax.optimization_barrier((blended, [moved[rel] for rel in early]))
            moved.update(zip(early, kept))
        backs.extend([outs[0]] + [moved[rel] for rel in range(1, peers)])
    if full:
        results.append(lax.all_to_all(blended, DEVICES, split_axis=0, concat_axis=0, tiled=True))
    results.extend(backs)
    return unpack(results, head_axis, start, each, full, chunks, devices, width)


def solution(mesh):
    rows = P(DEVICES, None)
    placed = (rows, rows, rows, P("seq", None), P("seq"))
    return jax.shard_map(body, mesh=mesh, in_specs=placed, out_specs=rows, check_vma=False)
```
